256 devices in a mesh: ctx: 64 (over z, y_hi, x), tp: 4 (over y_lo, core).
Axes of the slice: x: 4, y: 4 (y_hi: 2, y_lo: 2; y = y_hi * 2 + y_lo), z: 8, core: 2. Of those that a mesh axis runs over, the one named last changes fastest.
Arguments:
- span_q: bfloat16 [8192, 32, 128], P('ctx', 'tp'), may hold values from -104 to 104
- cache_kv: bfloat16 [8192, 8, 2, 128], P('ctx', 'tp'), may hold values from -4 to 4
- span_kv: bfloat16 [8192, 8, 2, 128], P('ctx', 'tp'), may hold values from -4 to 4
- span_blocks: int32 [64], replicated, may hold values from 0 to 63, each once
- parked_pages: bfloat16 [4096, 8, 8, 2, 128], P('ctx', None, 'tp'), may hold values from -4 to 4
- page_dest: int32 [4096, 1], replicated, may hold values from 0 to 63; in each aligned block of 64 rows (0 to 63, 64 to 127, ...) at most 2 rows name the same one
- page_req: int32 [4096], replicated, may hold values from 0 to 3
- decode_cache: bfloat16 [256, 512, 8, 2, 128], P('ctx', None, 'tp'), may hold values from -4 to 4
- decode_lengths: int32 [256], P('ctx'), may hold values from 1 to 512, 65536 in all
- decode_q: bfloat16 [256, 4, 32, 128], P('ctx', None, 'tp'), may hold values from -104 to 104
- decode_kv: bfloat16 [256, 4, 8, 2, 128], P('ctx', None, 'tp'), may hold values from -4 to 4
- out_weight: bfloat16 [32, 128, 4096], P('tp'), may hold values from -0.09375 to 0.09375
Outputs:
- prefill_out: bfloat16 [8192, 4096], P(('ctx', 'tp'))
- decode_out: bfloat16 [256, 4, 4096], P(('ctx', 'tp'))
The draws below stay inside these ranges and needn't reach their ends.
Inputs may be any that keep to these rules, and one draw needn't show every extreme that they name: `page_dest`: at most 2 of the 64 pages of one index of ctx name the same destination.
All inputs are finite; a program needn't handle non-finite values. No bound on the sum of `decode_lengths` on one device may be relied on, other than what follows from the above.
Results may differ from the reference program's by a relative error of at most 0.015.
Values may be sent and summed in bfloat16 or wider, within the bound.
A program may use at most 128 MiB of HBM per device.

```python
import math
import jax
import jax.numpy as jnp
import numpy as np
from jax import lax

D = 4096
H = 32
KVH = 8
HD = 128
CH_DEV = 128
PAGE = 8
PG_DEV = 64
REQ_DEV = 4
STEPS = 4
DLEN = 512
SPAN = 8192
CTX = 8192
REQUESTS = 256
TOTAL_PAGES = 4096
MOST = 2
N_CTX = 64


def draw_span_q(key, part):
    key = jax.random.fold_in(key, 1)
    shape = (SPAN, H, HD)
    values = jnp.clip(jax.random.normal(key, shape, jnp.float32) * 2.5, -10.0, 10.0)
    return values.astype(jnp.bfloat16)


def draw_decode_q(key, part):
    key = jax.random.fold_in(key, 2)
    shape = (REQUESTS, STEPS, H, HD)
    values = jnp.clip(jax.random.normal(key, shape, jnp.float32) * 2.5, -10.0, 10.0)
    return values.astype(jnp.bfloat16)


def plant(entries, stream_key, low, largest):
    extent = entries.shape
    place = [jax.random.randint(jax.random.fold_in(stream_key, axis), (), 0, extent[axis]) for axis in range(len(extent))]
    entries = entries.at[tuple(place)].set(low)
    longest = extent.index(max(extent))
    place[longest] = (place[longest] + 1) % extent[longest]
    return entries.at[tuple(place)].set(largest)


def block_levels(rng, dims, cuts, least, high):
    loudness = 1.0
    for axis_at, shards_of in cuts:
        steps = jax.random.uniform(jax.random.fold_in(jax.random.fold_in(rng, 6), axis_at), (shards_of,), jnp.float32, least / len(cuts), high / len(cuts))
        loudness = loudness * jnp.repeat(jnp.exp(steps), dims[axis_at] // shards_of).reshape((-1,) + (1,) * (len(dims) - 1 - axis_at))
    return loudness


def length_profile(number_of, total, reach, skew):
    weights = [(1 << 20) // math.isqrt(standing ** skew) + 1 for standing in range(2, number_of + 1)]
    rest, holding = total - reach - (number_of - 1), [1] * (number_of - 1)
    while rest > 0:
        movable = [i for i in range(number_of - 1) if holding[i] < reach]
        whole, budget = sum([weights[i] for i in movable]), rest
        for i in movable:
            more = min(reach - holding[i], max(1, budget * weights[i] // whole), rest)
            holding[i] = holding[i] + more
            rest = rest - more
    return np.array([reach] + holding)


def ragged_sizes(own_key, amount, total, reach, slope):
    if amount == 2:
        one = jax.random.randint(own_key, (), max(1, total - reach), min(reach, total - 1) + 1)
        return jnp.stack([one, total - one])
    tallies = jnp.asarray(length_profile(amount, total, reach, slope), jnp.int32)
    couples = (amount - 1) // 2
    donor, taker = tallies[1:1 + 2 * couples:2], tallies[2:2 + 2 * couples:2]
    slack = jnp.minimum(donor - 1, reach - taker)
    moved = jax.random.randint(jax.random.fold_in(own_key, 1), (couples,), 0, 1 << 20) % (slack + 1)
    tallies = tallies.at[1:1 + 2 * couples:2].set(donor - moved).at[2:2 + 2 * couples:2].set(taker + moved)
    return tallies[jax.random.permutation(jax.random.fold_in(own_key, 2), amount)]


def routed_block(rng, own, number, rows, amount, top, limit, skew):
    order = jax.random.permutation(rng, amount)
    heavy_load, usual = shares(amount, rows * top, limit, skew, True), shares(amount, rows * top, limit, skew, False)
    places = jnp.arange(amount)

    def named(sizes, rotation):
        used = int((sizes > 0).sum())
        fixed = max(1, used // 4)
        shifted = fixed + (places - fixed + rotation * (used - fixed)) % max(1, amount - fixed)
        return jnp.zeros((amount,), jnp.int32).at[order[jnp.where(places < fixed, places, shifted)]].set(jnp.asarray(sizes, jnp.int32))

    sizes = jnp.where(number % 4 == 0, named(heavy_load, number // 4), named(usual, number - number // 4 - 1))
    mixed = jax.random.permutation(jax.random.fold_in(own, 3), amount)
    source_of, receiver = mixed[0:amount // 2 * 2:2], mixed[1:amount // 2 * 2:2]
    slack = jnp.minimum(sizes[source_of] - 1, limit - sizes[receiver]) // 2
    slack = jnp.where((source_of == order[0]) | (receiver == order[0]) | (sizes[receiver] == 0), 0, jnp.maximum(slack, 0))
    shifted = jax.random.randint(jax.random.fold_in(own, 4), (amount // 2,), 0, 1 << 20) % (slack + 1)
    sizes = sizes.at[source_of].add(-shifted).at[receiver].add(shifted)
    labels = jnp.searchsorted(jnp.cumsum(sizes), jnp.arange(rows * top), side="right").astype(jnp.int32)
    listing = labels.reshape(top, rows).T
    listing = listing[jax.random.permutation(jax.random.fold_in(own, 1), rows)]
    rotation = jax.random.randint(jax.random.fold_in(own, 2), (rows, 1), 0, top)
    return jnp.take_along_axis(listing, (jnp.arange(top)[None, :] + rotation) % top, axis=1)


def shares(amount, total, bound, skew, full):
    weights = [(1 << 20) // math.isqrt(standing ** skew) + 1 for standing in range(1, amount + 1)]
    largest = bound if full else min(bound, max(-(-total // amount), total * weights[0] // sum(weights)))
    least = 1 if total - largest >= amount - 1 else 0
    given, rest = [largest] + [least] * (amount - 1), total - largest - least * (amount - 1)
    while rest > 0:
        candidates = [i for i in range(1, amount) if given[i] < largest] or [i for i in range(1, amount) if given[i] < bound]
        mass, budget = sum([weights[i] for i in candidates]), rest
        for i in candidates:
            extra = min(bound - given[i], max(1, budget * weights[i] // mass), rest)
            given[i] = given[i] + extra
            rest = rest - extra
    return np.array(given)


def normal_values(stream_key, dims, width, limit, pieces=(), held_as=jnp.bfloat16):
    result = jax.random.normal(stream_key, dims, jnp.float32) * width
    if len(pieces) > 0:
        result = block_levels(stream_key, dims, pieces, -0.22, 0.18) * result
    return jnp.clip(result, min=-limit, max=limit).astype(held_as)


def setup_inputs(seed: int = 0) -> dict:
    streams_of = jax.random.split(jax.random.key(seed), 13)
    span_q = draw_span_q(jax.random.fold_in(streams_of[12], 71), 0)
    cache_kv = normal_values(streams_of[1], (CTX, KVH, 2, HD), 1.0, 4.0, ((0, 64), (1, 4)))
    span_kv = normal_values(streams_of[2], (SPAN, KVH, 2, HD), 1.0, 4.0, ((0, 64), (1, 4)))
    span_blocks = jax.random.permutation(streams_of[3], N_CTX).astype(jnp.int32)
    parked_pages = normal_values(streams_of[4], (TOTAL_PAGES, PAGE, KVH, 2, HD), 1.0, 4.0, ((0, 64), (2, 4)))
    page_dest_keys = jax.random.split(jax.random.fold_in(streams_of[5], 1), TOTAL_PAGES // PG_DEV)
    page_dest_turns = jax.random.permutation(jax.random.fold_in(streams_of[5], 3), TOTAL_PAGES // PG_DEV)
    page_dest = jax.vmap(lambda own, number: routed_block(jax.random.fold_in(streams_of[5], 2), own, number, PG_DEV, N_CTX, 1, MOST, 2))(page_dest_keys, page_dest_turns).reshape((TOTAL_PAGES, 1))
    page_req = plant(jax.random.randint(streams_of[6], (TOTAL_PAGES,), 0, REQ_DEV), jax.random.fold_in(streams_of[6], 1), 0, REQ_DEV - 1).astype(jnp.int32)
    decode_cache = normal_values(streams_of[7], (REQUESTS, DLEN, KVH, 2, HD), 1.0, 4.0, ((0, 64), (2, 4)))
    decode_lengths = ragged_sizes(streams_of[8], REQUESTS, REQUESTS * DLEN // 2, DLEN, 2).astype(jnp.int32)
    decode_q = draw_decode_q(jax.random.fold_in(streams_of[12], 71), 0)
    decode_kv = normal_values(streams_of[10], (REQUESTS, STEPS, KVH, 2, HD), 1.0, 4.0, ((0, 64), (2, 4)))
    out_weight = normal_values(streams_of[11], (H, HD, D), (H * HD) ** -0.5, 0.09375, ((0, 4),))
    return {"span_q": span_q, "cache_kv": cache_kv, "span_kv": span_kv, "span_blocks": span_blocks, "parked_pages": parked_pages, "page_dest": page_dest, "page_req": page_req, "decode_cache": decode_cache, "decode_lengths": decode_lengths, "decode_q": decode_q, "decode_kv": decode_kv, "out_weight": out_weight}


NEG = -1e30


def attend(queries, parts):
    queries = queries.astype(jnp.float32)
    score_list = []
    for key_rows, value_rows, visible in parts:
        scores = jnp.einsum("mgd,kd->mgk", queries, key_rows.astype(jnp.float32)) * (HD ** -0.5)
        score_list.append(jnp.where(visible[:, None, :], scores, NEG))
    peak = jnp.max(score_list[0], axis=-1)
    for scores in score_list[1:]:
        peak = jnp.maximum(peak, jnp.max(scores, axis=-1))
    denominator = jnp.zeros(peak.shape, jnp.float32)
    numerator = jnp.zeros(peak.shape + (HD,), jnp.float32)
    for scores, part in zip(score_list, parts):
        visible = part[2]
        weights = jnp.where(visible[:, None, :], jnp.exp(scores - peak[..., None]), 0.0)
        denominator = denominator + jnp.sum(weights, axis=-1)
        rounded = weights.astype(jnp.bfloat16).astype(jnp.float32)
        numerator = numerator + jnp.einsum("mgk,kd->mgd", rounded, part[1].astype(jnp.float32))
    return (numerator / denominator[..., None]).astype(jnp.bfloat16)


def reference(span_q, cache_kv, span_kv, span_blocks, parked_pages, page_dest, page_req, decode_cache, decode_lengths, decode_q, decode_kv, out_weight):
    group_size = H // KVH
    row_ids = jnp.arange(SPAN, dtype=jnp.int32)
    query_pos = span_blocks[row_ids // CH_DEV] * CH_DEV + row_ids % CH_DEV

    def one_block(block_index):
        first_row = block_index * CH_DEV
        queries = lax.dynamic_slice_in_dim(span_q, first_row, CH_DEV, 0)
        own_pos = lax.dynamic_slice_in_dim(query_pos, first_row, CH_DEV, 0)
        cache_seen = jnp.ones((CH_DEV, CTX), dtype=bool)
        span_seen = query_pos[None, :] <= own_pos[:, None]
        grouped = queries.reshape(CH_DEV, KVH, group_size, HD)
        results = []
        for head_kv in range(KVH):
            parts = [(cache_kv[:, head_kv, 0], cache_kv[:, head_kv, 1], cache_seen),
                     (span_kv[:, head_kv, 0], span_kv[:, head_kv, 1], span_seen)]
            results.append(attend(grouped[:, head_kv], parts))
        return jnp.stack(results, axis=1).reshape(CH_DEV, H * HD)

    prefill_attn = lax.map(one_block, jnp.arange(N_CTX, dtype=jnp.int32)).reshape(SPAN, H * HD)

    page_rows = parked_pages.reshape(TOTAL_PAGES * PAGE, KVH, 2, HD)
    page_owner = page_dest[:, 0] * REQ_DEV + page_req
    key_owner = jnp.repeat(page_owner, PAGE)
    step_ids = jnp.arange(STEPS, dtype=jnp.int32)
    slot_ids = jnp.arange(DLEN, dtype=jnp.int32)

    def one_request(request):
        resident = decode_cache[request]
        fresh = decode_kv[request]
        seen_res = jnp.broadcast_to(slot_ids[None, :] < decode_lengths[request], (STEPS, DLEN))
        seen_page = jnp.broadcast_to((key_owner == request)[None, :], (STEPS, TOTAL_PAGES * PAGE))
        seen_new = step_ids[None, :] <= step_ids[:, None]
        grouped = decode_q[request].reshape(STEPS, KVH, group_size, HD)
        results = []
        for head_kv in range(KVH):
            parts = [(resident[:, head_kv, 0], resident[:, head_kv, 1], seen_res),
                     (page_rows[:, head_kv, 0], page_rows[:, head_kv, 1], seen_page),
                     (fresh[:, head_kv, 0], fresh[:, head_kv, 1], seen_new)]
            results.append(attend(grouped[:, head_kv], parts))
        return jnp.stack(results, axis=1).reshape(STEPS, H * HD)

    decode_attn = lax.map(one_request, jnp.arange(REQUESTS, dtype=jnp.int32))
    weight = out_weight.reshape(H * HD, D)
    prefill_out = jnp.dot(prefill_attn, weight, preferred_element_type=jnp.float32).astype(jnp.bfloat16)
    decode_out = jnp.dot(decode_attn.reshape(REQUESTS * STEPS, H * HD), weight, preferred_element_type=jnp.float32)
    decode_out = decode_out.astype(jnp.bfloat16).reshape(REQUESTS, STEPS, D)
    return prefill_out, decode_out
```

```python
import functools

import jax
import jax.numpy as jnp
from jax import lax
from jax.experimental import pallas as pl
from jax.experimental.pallas import tpu as pltpu
from jax.sharding import PartitionSpec as P

NEG = -1e30
LOG2E = 1.4426950408889634
MESH = pl.DeviceIdType.MESH
BF16 = jnp.bfloat16
F32 = jnp.float32
NT = (((1,), (1,)), ((), ()))

NZ, NR = 8, 8
TOK = 128
HD = 128
GROUP = 4
QROWS = GROUP * TOK
KEYS = 2 * TOK * NZ
COLS = 1024
CHUNKS = 4
PAGE_ROWS = 32
POOL = 4096


def remote(src, dst, send, recv, **device):
    return pltpu.make_async_remote_copy(
        src_ref=src, dst_ref=dst, send_sem=send, recv_sem=recv, device_id=device, device_id_type=MESH
    )


def fold8(x):
    return jnp.max(x.reshape(x.shape[0] // 8, 8, x.shape[1]), axis=0)


def kernel(
    blocks_ref, page_ix_ref, lens_ref, q_in, kv_in, pages_in, owner_ref, cache_in, dq_ref, dkv_ref, w_in,
    out_ref, dout_ref,
    kvbuf, qbuf, s_ref, obuf, orecv, stbuf, strecv, dbias, pages, pg_out, pool, dcache, wbuf,
    lhs, pbuf, rbuf, sbuf, tbuf, pdec, rdec, sdec, tdec,
    lsem, kv_s, kv_r, q_s, q_r, o_s, o_r, st_s, st_r, pg_s, pg_r, t1_s, t1_r, t2_s, t2_r,
):
    me = lax.axis_index("ctx")
    tp = lax.axis_index("tp")
    z = me // NR
    rest = me % NR
    score_c = (HD ** -0.5) * LOG2E

    barrier = pltpu.get_barrier_semaphore()

    def greet(k, _):
        pl.semaphore_signal(barrier, inc=1, device_id={"ctx": (me + k) % 64}, device_id_type=MESH)
        return 0

    lax.fori_loop(1, 64, greet, 0)
    for k in range(1, 4):
        pl.semaphore_signal(barrier, inc=1, device_id={"tp": (tp + k) % 4}, device_id_type=MESH)

    local = [
        pltpu.make_async_copy(kv_in, kvbuf.at[:, 0], lsem.at[0]),
        pltpu.make_async_copy(q_in, qbuf.at[0], lsem.at[1]),
        pltpu.make_async_copy(pages_in, pages, lsem.at[2]),
        pltpu.make_async_copy(cache_in, dcache, lsem.at[3]),
        pltpu.make_async_copy(w_in, wbuf, lsem.at[4]),
    ]
    for copy in local:
        copy.start()
    local[0].wait()
    local[1].wait()
    pl.semaphore_wait(barrier, 66)

    q_copies = []
    for k in range(1, NR):
        copy = remote(
            qbuf.at[0], qbuf.at[k], q_s.at[k], q_r.at[k], ctx=z * NR + (rest + k) % NR
        )
        copy.start()
        q_copies.append(copy)

    ring = {}
    order = []
    for t in range(4):
        for half in range(2):
            for way in range(2):
                if t == 3 and half != way:
                    continue
                here = (-t) % NZ if way == 0 else t
                there = (-t - 1) % NZ if way == 0 else t + 1
                to = (z + 1) % NZ if way == 0 else (z + NZ - 1) % NZ
                ring[t, half, way] = remote(
                    kvbuf.at[:, here, half], kvbuf.at[:, there, half],
                    kv_s.at[way, t, half], kv_r.at[way, t, half], ctx=to * NR + rest,
                )
                order.append((t, half, way))
    for key in order:
        if key[0] == 0:
            ring[key].start()

    local[2].wait()

    def place(t, _):
        for i in range(2):
            pg_out[t, i * PAGE_ROWS : (i + 1) * PAGE_ROWS, :] = pages[page_ix_ref[t * 2 + i]]
        return 0

    lax.fori_loop(0, 64, place, 0)

    local[3].wait()
    row = lax.broadcasted_iota(jnp.int32, (128, 128), 0)
    lane = lax.broadcasted_iota(jnp.int32, (128, 128), 1)
    perm = (lane == (row % 16) * 8 + row // 16).astype(BF16)
    dq = jnp.dot(perm, dq_ref[...], preferred_element_type=F32).astype(BF16)
    col_req = (lax.broadcasted_iota(jnp.int32, (128, 1), 0) // 4) % 4
    col_step = lax.broadcasted_iota(jnp.int32, (128, 1), 0) % 4
    col_head = lax.broadcasted_iota(jnp.int32, (128, 1), 0) // 64
    length = jnp.zeros((128, 1), jnp.int32)
    for r in range(4):
        length = jnp.where(col_req == r, lens_ref[r], length)

    def weigh(scores):
        m = jnp.max(scores, axis=1, keepdims=True)
        p = jnp.exp2(scores * score_c - m * score_c)
        total = jnp.sum(p, axis=1, keepdims=True)
        return m * score_c, total, pltpu.roll(p, 1, 1).astype(BF16)

    wide = jnp.concatenate([dcache[r * 2048 : (r + 1) * 2048, :] for r in range(4)], axis=1)
    zero = jnp.zeros((), BF16)
    dq_wide = jnp.concatenate([jnp.where(col_req == r, dq, zero) for r in range(4)], axis=1)
    res = lax.dot_general(dq_wide, wide, NT, preferred_element_type=F32)
    at = lax.broadcasted_iota(jnp.int32, (1, 2048), 1)
    res = jnp.where((at // 4 < length) & (at % 4 == col_head * 2), res, NEG)
    new = lax.dot_general(dq, dkv_ref[...], NT, preferred_element_type=F32)
    at = lax.broadcasted_iota(jnp.int32, (1, 64), 1)
    new = jnp.where(
        (at // 16 == col_req) & ((at // 4) % 4 <= col_step) & (at % 4 == col_head * 2), new, NEG
    )
    new = jnp.concatenate([new, jnp.full((128, 64), NEG, F32)], axis=1)
    res_m, res_l, res_p = weigh(jnp.concatenate([res, new], axis=1))
    part = jnp.dot(res_p[:, :2048], wide, preferred_element_type=F32)
    res_o = jnp.dot(res_p[:, 2048:2112], dkv_ref[...], preferred_element_type=F32)
    for r in range(4):
        res_o = res_o + jnp.where(col_req == r, part[:, r * HD : (r + 1) * HD], 0.0)

    for key in order:
        t, half, way = key
        if t > 0:
            ring[t - 1, half, way].wait_recv()
            ring[key].start()
    for key in order:
        t, half, way = key
        if t == 3 or (t == 2 and half != way):
            ring[key].wait_recv()
    for copy in q_copies:
        copy.wait_recv()

    own_pages = pltpu.make_async_copy(pg_out.at[me], pool.at[me], lsem.at[5])
    own_pages.start()

    def page_copy(k):
        to = (me + k) % 64
        return remote(pg_out.at[to], pool.at[me], pg_s.at[k], pg_r.at[k], ctx=to)

    def page_start(k, _):
        page_copy(k).start()
        return 0

    lax.fori_loop(1, 64, page_start, 0)

    def scores(k, head, slot):
        keys = kvbuf[head].reshape(KEYS, HD)
        s_ref[slot] = lax.dot_general(keys, qbuf[k % NR, head], NT, preferred_element_type=F32)

    def attend(k, head, slot):
        at_q = z * NR + (rest + 2 * NR - k) % NR
        q_pos = blocks_ref[at_q]
        hide = []
        peak = None
        for d in range(NZ):
            k_pos = blocks_ref[((z + d) % NZ) * NR + rest]
            hide.append(jnp.minimum(q_pos - k_pos, 0).astype(F32) * -NEG)
            first = d * 2 * TOK
            top = fold8(s_ref[slot, first : first + TOK, :])
            peak = top if peak is None else jnp.maximum(peak, top)
            if d == 0:
                s_ref[slot, TOK : 2 * TOK, :] = s_ref[slot, TOK : 2 * TOK, :] + dbias[...]
            top = fold8(s_ref[slot, first + TOK : first + 2 * TOK, :])
            peak = jnp.maximum(peak, top + hide[d])
        m = jnp.max(peak, axis=0, keepdims=True) * score_c
        weights = []
        values = []
        for d in range(NZ):
            first = d * 2 * TOK
            weights.append(jnp.exp2(s_ref[slot, first : first + TOK, :] * score_c - m).astype(BF16))
            shift = m - hide[d]
            weights.append(
                jnp.exp2(s_ref[slot, first + TOK : first + 2 * TOK, :] * score_c - shift).astype(BF16)
            )
            values.append(kvbuf[2 + head, d, 0])
            values.append(kvbuf[2 + head, d, 1])
        values = jnp.concatenate(values, axis=1)
        values = jnp.concatenate([values, jnp.ones((16, KEYS), BF16)], axis=0)
        o = jnp.dot(values, jnp.concatenate(weights, axis=0), preferred_element_type=F32)
        total = o[HD : HD + 1]
        obuf[k % NR, head] = (o[:HD] * (1.0 / total)).astype(BF16)
        lse = m + jnp.log2(total)
        for g in range(GROUP):
            stbuf[k % NR, head * GROUP + g : head * GROUP + g + 1, :] = lse[:, g * TOK : (g + 1) * TOK]

    def o_copy(k):
        to = z * NR + (rest + 2 * NR - k) % NR
        return remote(obuf.at[k], orecv.at[k], o_s.at[k], o_r.at[k], ctx=to)

    def st_copy(k):
        to = z * NR + (rest + 2 * NR - k) % NR
        return remote(stbuf.at[k], strecv.at[k], st_s.at[k], st_r.at[k], ctx=to)

    dbias[...] = jnp.zeros_like(dbias)
    scores(1, 0, 0)

    def step(k, _):
        @pl.when(k == NR)
        def _():
            key_at = lax.broadcasted_iota(jnp.int32, (TOK, QROWS), 0)
            query_at = lax.broadcasted_iota(jnp.int32, (TOK, QROWS), 1) % TOK
            dbias[...] = jnp.where(key_at <= query_at, 0.0, NEG)

        scores(k, 1, 1)
        attend(k, 0, 0)
        scores(k + 1, 0, 0)
        attend(k, 1, 1)

        @pl.when(k < NR)
        def _():
            o_copy(k).start()
            st_copy(k).start()

        return 0

    lax.fori_loop(1, NR + 1, step, 0)

    def page_wait(k, _):
        source = (me + 64 - k) % 64
        to = (me + k) % 64
        remote(pg_out.at[to], pool.at[source], pg_s.at[k], pg_r.at[k], ctx=to).wait()
        return 0

    lax.fori_loop(1, 64, page_wait, 0)
    own_pages.wait()
    pool_rows = pool[...].reshape(POOL, HD)
    found = lax.dot_general(dq, pool_rows, NT, preferred_element_type=F32)
    at = lax.broadcasted_iota(jnp.int32, (1, POOL), 1)
    found = jnp.where((owner_ref[...] == col_req) & (at % 4 == col_head * 2), found, NEG)
    pool_m, pool_l, pool_p = weigh(found)
    pool_o = jnp.dot(pool_p, pool_rows, preferred_element_type=F32)
    both = jnp.maximum(res_m, pool_m)
    res_a = jnp.exp2(res_m - both)
    pool_a = jnp.exp2(pool_m - both)
    dec = (res_o * res_a + pool_o * pool_a) / (res_l * res_a + pool_l * pool_a)
    for h in range(8):
        lhs[TOK : TOK + 16, h * HD : (h + 1) * HD] = dec[h * 16 : (h + 1) * 16, :].astype(BF16)

    for k in range(1, NR):
        remote(
            obuf.at[k], orecv.at[k], o_s.at[k], o_r.at[k], ctx=z * NR + (rest + NR - k) % NR
        ).wait()
        remote(
            stbuf.at[k], strecv.at[k], st_s.at[k], st_r.at[k], ctx=z * NR + (rest + NR - k) % NR
        ).wait()
    lse = [stbuf[0]] + [strecv[k] for k in range(1, NR)]
    top = functools.reduce(jnp.maximum, lse)
    share = [jnp.exp2(x - top) for x in lse]
    whole = 1.0 / functools.reduce(jnp.add, share)
    share = [x * whole for x in share]
    for h in range(8):
        head, g = h // GROUP, h % GROUP
        cols = slice(g * TOK, (g + 1) * TOK)
        merged = obuf[0, head, :, cols].astype(F32) * share[0][h : h + 1]
        for k in range(1, NR):
            merged = merged + orecv[k, head, :, cols].astype(F32) * share[k][h : h + 1]
        lhs[:TOK, h * HD : (h + 1) * HD] = merged.T.astype(BF16)

    core = tp % 2
    side = tp // 2
    sibling = side * 2 + (1 - core)
    across = (1 - side) * 2 + core
    local[4].wait()

    def first_copy(c):
        if c == CHUNKS:
            return remote(pdec.at[:, 1 - core], rdec, t1_s.at[c], t1_r.at[c], tp=sibling)
        return remote(pbuf.at[c, :, 1 - core], rbuf.at[c], t1_s.at[c], t1_r.at[c], tp=sibling)

    def second_copy(c):
        if c == CHUNKS:
            return remote(sdec, tdec, t2_s.at[c], t2_r.at[c], tp=across)
        return remote(sbuf.at[c], tbuf.at[c], t2_s.at[c], t2_r.at[c], tp=across)

    def second(c):
        first_copy(c).wait_recv()
        if c == CHUNKS:
            sdec[...] = (
                pdec[1 - side, core].astype(F32) + rdec[1 - side].astype(F32)
            ).astype(BF16)
        else:
            sbuf[c] = (
                pbuf[c, 1 - side, core].astype(F32) + rbuf[c, 1 - side].astype(F32)
            ).astype(BF16)
        second_copy(c).start()

    dec_parts = []
    for c in range(CHUNKS):
        part = jnp.dot(lhs[...], wbuf[:, c * COLS : (c + 1) * COLS], preferred_element_type=F32)
        pbuf[c] = part[:TOK].astype(BF16).reshape(2, 2, TOK // 4, COLS)
        dec_parts.append(part[TOK:])
        first_copy(c).start()
        if c > 0:
            second(c - 1)
    for t in range(4):
        rows = jnp.concatenate([part[t * 4 : (t + 1) * 4] for part in dec_parts], axis=0)
        pdec[t // 2, t % 2] = rows.astype(BF16)
    first_copy(CHUNKS).start()
    second(CHUNKS - 1)
    second(CHUNKS)
    for c in range(CHUNKS):
        second_copy(c).wait_recv()
        out_ref[:, c * COLS : (c + 1) * COLS] = (
            pbuf[c, side, core].astype(F32) + rbuf[c, side].astype(F32) + tbuf[c].astype(F32)
        ).astype(BF16)
    second_copy(CHUNKS).wait_recv()
    rows = pdec[side, core].astype(F32) + rdec[side].astype(F32) + tdec[...].astype(F32)
    dout_ref[...] = jnp.concatenate(
        [rows[c * 4 : (c + 1) * 4] for c in range(CHUNKS)], axis=1
    ).astype(BF16)

    for key in order:
        ring[key].wait_send()
    for copy in q_copies:
        copy.wait_send()
    for c in range(CHUNKS + 1):
        first_copy(c).wait_send()
        second_copy(c).wait_send()


def body(
    span_q, cache_kv, span_kv, span_blocks, parked_pages, page_dest, page_req,
    decode_cache, decode_lengths, decode_q, decode_kv, out_weight,
):
    me = lax.axis_index("ctx")
    q = span_q.reshape(TOK, 2, GROUP, HD).transpose(1, 2, 0, 3).reshape(2, QROWS, HD)
    kv = jnp.stack([cache_kv, span_kv], axis=0)
    keys = kv[:, :, :, 0].transpose(2, 0, 1, 3)
    values = kv[:, :, :, 1].transpose(2, 0, 3, 1)
    kv = jnp.concatenate([keys, values], axis=0)
    pages = parked_pages.reshape(64, PAGE_ROWS, HD)

    targets = page_dest[:, 0].reshape(64, 64)
    own = lax.dynamic_index_in_dim(targets, me, 0, keepdims=False)
    slot = jnp.arange(64, dtype=jnp.int32)
    hit = own[None, :] == slot[:, None]
    first = jnp.min(jnp.where(hit, slot[None, :], 63), axis=1)
    last = jnp.max(jnp.where(hit, slot[None, :], 0), axis=1)
    page_ix = jnp.stack([first, last], axis=1).reshape(128)
    code = slot[None, :] * 4 + page_req.reshape(64, 64)
    here = targets == me
    low = jnp.min(jnp.where(here, code, 1 << 20), axis=1)
    high = jnp.max(jnp.where(here, code, -1), axis=1)
    owner = jnp.stack(
        [jnp.where(high >= 0, low % 4, -1), jnp.where(high > low, high % 4, -1)], axis=1
    )
    owner = jnp.broadcast_to(owner[:, :, None], (64, 2, PAGE_ROWS)).reshape(1, POOL)

    smem = pl.BlockSpec(memory_space=pltpu.SMEM)
    vmem = pl.BlockSpec(memory_space=pltpu.VMEM)
    hbm = pl.BlockSpec(memory_space=pl.ANY)
    dma = pltpu.SemaphoreType.DMA
    out, dout = pl.pallas_call(
        kernel,
        name="layer",
        out_shape=[
            jax.ShapeDtypeStruct((TOK // 4, CHUNKS * COLS), BF16),
            jax.ShapeDtypeStruct((4, CHUNKS * COLS), BF16),
        ],
        in_specs=[smem, smem, smem, hbm, hbm, hbm, vmem, hbm, vmem, vmem, hbm],
        out_specs=[vmem, vmem],
        scratch_shapes=[
            pltpu.VMEM((4, NZ, 2, HD, HD), BF16),
            pltpu.VMEM((NR, 2, QROWS, HD), BF16),
            pltpu.VMEM((2, KEYS, QROWS), F32),
            pltpu.VMEM((NR, 2, HD, QROWS), BF16),
            pltpu.VMEM((NR, 2, HD, QROWS), BF16),
            pltpu.VMEM((NR, 8, TOK), F32),
            pltpu.VMEM((NR, 8, TOK), F32),
            pltpu.VMEM((TOK, QROWS), F32),
            pltpu.VMEM((64, PAGE_ROWS, HD), BF16),
            pltpu.VMEM((64, 2 * PAGE_ROWS, HD), BF16),
            pltpu.VMEM((64, 2 * PAGE_ROWS, HD), BF16),
            pltpu.VMEM((4 * 2048, HD), BF16),
            pltpu.VMEM((8 * HD, CHUNKS * COLS), BF16),
            pltpu.VMEM((TOK + 16, 8 * HD), BF16),
            pltpu.VMEM((CHUNKS, 2, 2, TOK // 4, COLS), BF16),
            pltpu.VMEM((CHUNKS, 2, TOK // 4, COLS), BF16),
            pltpu.VMEM((CHUNKS, TOK // 4, COLS), BF16),
            pltpu.VMEM((CHUNKS, TOK // 4, COLS), BF16),
            pltpu.VMEM((2, 2, 16, COLS), BF16),
            pltpu.VMEM((2, 16, COLS), BF16),
            pltpu.VMEM((16, COLS), BF16),
            pltpu.VMEM((16, COLS), BF16),
            dma((6,)),
            dma((2, 4, 2)), dma((2, 4, 2)),
            dma((NR,)), dma((NR,)),
            dma((NR,)), dma((NR,)),
            dma((NR,)), dma((NR,)),
            dma((64,)), dma((64,)),
            dma((CHUNKS + 1,)), dma((CHUNKS + 1,)),
            dma((CHUNKS + 1,)), dma((CHUNKS + 1,)),
        ],
        compiler_params=pltpu.CompilerParams(
            collective_id=0, has_side_effects=True, vmem_limit_bytes=56 << 20
        ),
    )(
        span_blocks, page_ix, decode_lengths, q, kv, pages, owner,
        decode_cache.reshape(4 * 2048, HD), decode_q.reshape(128, HD), decode_kv.reshape(64, HD),
        out_weight.reshape(8 * HD, CHUNKS * COLS),
    )
    return out, dout.reshape(1, 4, CHUNKS * COLS)


def solution(mesh):
    return jax.shard_map(
        body,
        mesh=mesh,
        in_specs=(
            P("ctx", "tp", None),
            P("ctx", "tp", None, None),
            P("ctx", "tp", None, None),
            P(),
            P("ctx", None, "tp", None, None),
            P(),
            P(),
            P("ctx", None, "tp", None, None),
            P("ctx"),
            P("ctx", None, "tp", None),
            P("ctx", None, "tp", None, None),
            P("tp", None, None),
        ),
        out_specs=(P(("ctx", "tp"), None), P(("ctx", "tp"), None, None)),
        check_vma=False,
    )
```

```python
import functools

import jax
import jax.numpy as jnp
from jax import lax
from jax.experimental import pallas as pl
from jax.experimental.pallas import tpu as pltpu
from jax.sharding import PartitionSpec as P

NEG = -1e30
LOG2E = 1.4426950408889634
MESH = pl.DeviceIdType.MESH
BF16 = jnp.bfloat16
F32 = jnp.float32
NT = (((1,), (1,)), ((), ()))

NZ, NR = 8, 8
TOK = 128
HD = 128
GROUP = 4
QROWS = GROUP * TOK
PHASES = ((0, 1, 7), (2, 6, 3, 5, 4))
MOST_KEYS = 5 * 2 * TOK
DX = (0, 0, 1, 3, 2, 1, 3, 2)
DY = (0, 1, 0, 0, 0, 1, 1, 1)
COLS = 1024
CHUNKS = 4
PAGE_ROWS = 32
POOL = 4096


def remote(src, dst, send, recv, **device):
    return pltpu.make_async_remote_copy(
        src_ref=src, dst_ref=dst, send_sem=send, recv_sem=recv, device_id=device, device_id_type=MESH
    )


def fold8(x):
    return jnp.max(x.reshape(x.shape[0] // 8, 8, x.shape[1]), axis=0)


def kernel(
    blocks_ref, lens_ref, q_in, cache_in, span_in, pages_in, dest_in, req_in, dcache_in, dq_in, dkv_in, w_in,
    out_ref, dout_ref,
    q_raw, kv_raw, dest, req, dq_raw, dkv, page_ix, page_at, hide,
    kvbuf, qbuf, s_ref, acc, peaks, obuf, orecv, stbuf, strecv, pages, pg_out, pool, dcache, wbuf,
    lhs, pbuf, rbuf, sbuf, tbuf, pdec, rdec, sdec, tdec,
    lsem, kv_s, kv_r, q_s, q_r, o_s, o_r, st_s, st_r, pg_s, pg_r, t1_s, t1_r, t2_s, t2_r,
):
    me = lax.axis_index("ctx")
    tp = lax.axis_index("tp")
    z = me // NR
    rest = me % NR
    y = rest // 4
    x = rest % 4
    score_c = (HD ** -0.5) * LOG2E

    def plane(dx, dy):
        return z * NR + ((y + dy) % 2) * 4 + (x + dx) % 4

    barrier = pltpu.get_barrier_semaphore()

    def greet(k, _):
        pl.semaphore_signal(barrier, inc=1, device_id={"ctx": (me + k) % 64}, device_id_type=MESH)
        return 0

    lax.fori_loop(1, 64, greet, 0)
    for k in range(1, 4):
        pl.semaphore_signal(barrier, inc=1, device_id={"tp": (tp + k) % 4}, device_id_type=MESH)

    moves = [
        (q_in, q_raw), (cache_in, kv_raw.at[0]), (span_in, kv_raw.at[1]), (dest_in, dest), (req_in, req),
        (pages_in, pages), (dq_in, dq_raw), (dkv_in, dkv), (dcache_in, dcache), (w_in, wbuf),
    ]
    local = [pltpu.make_async_copy(src, dst, lsem.at[i]) for i, (src, dst) in enumerate(moves)]
    for copy in local:
        copy.start()

    for k in range(NR):
        q_pos = blocks_ref[plane(4 - DX[k], DY[k])]
        for d in range(NZ):
            k_pos = blocks_ref[((z + d) % NZ) * NR + rest]
            hide[k * NZ + d] = jnp.minimum(q_pos - k_pos, 0).astype(F32) * -NEG

    row = lax.broadcasted_iota(jnp.int32, (128, 128), 0)
    lane = lax.broadcasted_iota(jnp.int32, (128, 128), 1)
    by_head = (lane == (row % 16) * 8 + row // 16).astype(BF16)
    by_kind = (lane == (row % 32) * 4 + row // 32).astype(BF16)
    local[0].wait()
    for b in range(8):
        part = jnp.dot(by_head, q_raw[b * 128 : (b + 1) * 128, :], preferred_element_type=F32)
        for h in range(8):
            at = (h % GROUP) * TOK + b * 16
            qbuf[0, h // GROUP, at : at + 16, :] = part[h * 16 : (h + 1) * 16].astype(BF16)
    local[1].wait()
    local[2].wait()
    for half in range(2):
        parts = [
            jnp.dot(by_kind, kv_raw[half, b * 128 : (b + 1) * 128, :], preferred_element_type=F32)
            for b in range(4)
        ]
        for h in range(2):
            first = h * 64
            keys = jnp.concatenate([part[first : first + 32] for part in parts], axis=0)
            values = jnp.concatenate([part[first + 32 : first + 64] for part in parts], axis=0)
            kvbuf[h, 0, half] = keys.astype(BF16)
            kvbuf[2 + h, 0, half] = values.T.astype(BF16)

    local[3].wait()
    own_row = dest[pl.ds(me // 2, 1), :]
    slot_lane = lax.broadcasted_iota(jnp.int32, (64, 128), 1)
    hit = (own_row == lax.broadcasted_iota(jnp.int32, (64, 128), 0)) & (slot_lane // 64 == me % 2)
    first = jnp.min(jnp.where(hit, slot_lane % 64, 63), axis=1, keepdims=True)
    last = jnp.max(jnp.where(hit, slot_lane % 64, 0), axis=1, keepdims=True)
    page_ix[...] = jnp.where(slot_lane < 64, first, last)
    to_smem = pltpu.make_async_copy(page_ix, page_at, lsem.at[10])
    to_smem.start()

    local[4].wait()
    code_lane = lax.broadcasted_iota(jnp.int32, (32, 128), 1)
    code = (code_lane % 64) * 4 + req[...]
    owners = [None] * 4
    for odd in range(2):
        hit = (dest[...] == me) & (code_lane // 64 == odd)
        low = jnp.min(jnp.where(hit, code, 1 << 20), axis=1, keepdims=True)
        high = jnp.max(jnp.where(hit, code, -1), axis=1, keepdims=True)
        owners[odd] = jnp.where(high >= 0, low % 4, -1)
        owners[2 + odd] = jnp.where(high > low, high % 4, -1)
    owner = jnp.concatenate(owners, axis=0)
    owned = (owner == (lane // 4) % 4).astype(BF16)
    to_smem.wait()

    pl.semaphore_wait(barrier, 66)

    def q_copy(k, head):
        if k < 5:
            src, to = 0, plane(DX[k], DY[k])
        elif head == 0:
            src, to = 1, plane(DX[k], 0)
        else:
            src, to = k - 3, plane(0, 1)
        return remote(qbuf.at[src, head], qbuf.at[k, head], q_s.at[k, head], q_r.at[k, head], ctx=to)

    def ring(t, half, way):
        here = (-t) % NZ if way == 0 else t
        there = (-t - 1) % NZ if way == 0 else t + 1
        to = (z + 1) % NZ if way == 0 else (z + NZ - 1) % NZ
        return remote(
            kvbuf.at[:, here, half], kvbuf.at[:, there, half],
            kv_s.at[way, t, half], kv_r.at[way, t, half], ctx=to * NR + rest,
        )

    def ring_step(t, half):
        for way in range(2):
            if t < 3 or half == way:
                if t > 0:
                    ring(t - 1, half, way).wait_recv()
                ring(t, half, way).start()

    q_copy(1, 0).start()
    ring_step(0, 0)
    for k in (2, 3, 4):
        q_copy(k, 1).start()
    ring_step(0, 1)
    for k in (2, 3, 4):
        q_copy(k, 0).start()
    q_copy(1, 1).start()

    local[5].wait()

    def place(t, _):
        for i in range(2):
            pg_out[t, i * PAGE_ROWS : (i + 1) * PAGE_ROWS, :] = pages[page_at[t, i * 64]]
        return 0

    lax.fori_loop(0, 64, place, 0)
    own_pages = pltpu.make_async_copy(pg_out.at[me], pool.at[me], lsem.at[11])
    own_pages.start()

    ring_step(1, 0)

    local[6].wait()
    local[7].wait()
    local[8].wait()
    dq = jnp.dot(by_head, dq_raw[...], preferred_element_type=F32).astype(BF16)
    col_req = (lax.broadcasted_iota(jnp.int32, (128, 1), 0) // 4) % 4
    col_step = lax.broadcasted_iota(jnp.int32, (128, 1), 0) % 4
    col_head = lax.broadcasted_iota(jnp.int32, (128, 1), 0) // 64
    length = jnp.zeros((128, 1), jnp.int32)
    for r in range(4):
        length = jnp.where(col_req == r, lens_ref[r], length)

    def weigh(scores):
        m = jnp.max(scores, axis=1, keepdims=True)
        p = jnp.exp2(scores * score_c - m * score_c)
        total = jnp.sum(p, axis=1, keepdims=True)
        return m * score_c, total, pltpu.roll(p, 1, 1).astype(BF16)

    wide = jnp.concatenate([dcache[r * 2048 : (r + 1) * 2048, :] for r in range(4)], axis=1)
    zero = jnp.zeros((), BF16)
    dq_wide = jnp.concatenate([jnp.where(col_req == r, dq, zero) for r in range(4)], axis=1)
    res = lax.dot_general(dq_wide, wide, NT, preferred_element_type=F32)
    at = lax.broadcasted_iota(jnp.int32, (1, 2048), 1)
    res = jnp.where((at // 4 < length) & (at % 4 == col_head * 2), res, NEG)
    new = lax.dot_general(dq, dkv[...], NT, preferred_element_type=F32)
    at = lax.broadcasted_iota(jnp.int32, (1, 64), 1)
    new = jnp.where(
        (at // 16 == col_req) & ((at // 4) % 4 <= col_step) & (at % 4 == col_head * 2), new, NEG
    )
    new = jnp.concatenate([new, jnp.full((128, 64), NEG, F32)], axis=1)
    res_m, res_l, res_p = weigh(jnp.concatenate([res, new], axis=1))
    part = jnp.dot(res_p[:, :2048], wide, preferred_element_type=F32)
    res_o = jnp.dot(res_p[:, 2048:2112], dkv[...], preferred_element_type=F32)
    for r in range(4):
        res_o = res_o + jnp.where(col_req == r, part[:, r * HD : (r + 1) * HD], 0.0)

    q_copy(1, 0).wait_recv()
    for k in (5, 6, 7):
        q_copy(k, 0).start()
    ring_step(1, 1)

    def scores(phase, k, head, slot):
        keys = jnp.concatenate([kvbuf[head, d].reshape(2 * TOK, HD) for d in PHASES[phase]], axis=0)
        s_ref[slot, : len(PHASES[phase]) * 2 * TOK, :] = lax.dot_general(
            keys, qbuf[k, head], NT, preferred_element_type=F32
        )

    def attend(phase, k, head, slot, own=False):
        peak = None if phase == 0 else peaks[k, head]
        shifts = []
        for i, d in enumerate(PHASES[phase]):
            cached = slice(i * 2 * TOK, (i * 2 + 1) * TOK)
            fresh = slice((i * 2 + 1) * TOK, (i * 2 + 2) * TOK)
            shifts.append(hide[k * NZ + d])
            top = fold8(s_ref[slot, cached, :])
            peak = top if peak is None else jnp.maximum(peak, top)
            if own and d == 0:
                key_at = lax.broadcasted_iota(jnp.int32, (TOK, QROWS), 0)
                query_at = lax.broadcasted_iota(jnp.int32, (TOK, QROWS), 1) % TOK
                s_ref[slot, fresh, :] = jnp.where(key_at <= query_at, s_ref[slot, fresh, :], NEG)
            peak = jnp.maximum(peak, fold8(s_ref[slot, fresh, :]) + shifts[-1])
        m = jnp.max(peak, axis=0, keepdims=True) * score_c
        weights = []
        values = []
        for i, d in enumerate(PHASES[phase]):
            cached = slice(i * 2 * TOK, (i * 2 + 1) * TOK)
            fresh = slice((i * 2 + 1) * TOK, (i * 2 + 2) * TOK)
            weights.append(jnp.exp2(s_ref[slot, cached, :] * score_c - m).astype(BF16))
            weights.append(jnp.exp2(s_ref[slot, fresh, :] * score_c - (m - shifts[i])).astype(BF16))
            values.append(kvbuf[2 + head, d, 0])
            values.append(kvbuf[2 + head, d, 1])
        values = jnp.concatenate(values, axis=1)
        values = jnp.concatenate([values, jnp.ones((16, values.shape[1]), BF16)], axis=0)
        o = jnp.dot(values, jnp.concatenate(weights, axis=0), preferred_element_type=F32)[: HD + 8]
        if phase == 0:
            acc[k, head] = o
            peaks[k, head] = peak
            return
        before = jnp.max(peaks[k, head], axis=0, keepdims=True) * score_c
        o = o + acc[k, head] * jnp.exp2(before - m)
        total = o[HD : HD + 1]
        obuf[k, head] = (o[:HD] * (1.0 / total)).astype(BF16)
        lse = m + jnp.log2(total)
        for g in range(GROUP):
            stbuf[k, head * GROUP + g : head * GROUP + g + 1, :] = lse[:, g * TOK : (g + 1) * TOK]

    def o_copy(k):
        return remote(obuf.at[k], orecv.at[k], o_s.at[k], o_r.at[k], ctx=plane(4 - DX[k], DY[k]))

    def st_copy(k):
        return remote(stbuf.at[k], strecv.at[k], st_s.at[k], st_r.at[k], ctx=plane(4 - DX[k], DY[k]))

    def step0(k, own=False):
        scores(0, k, 1, 1)
        attend(0, k, 0, 0, own)
        scores(0, (k + 1) % NR, 0, 0)
        attend(0, k, 1, 1, own)

    scores(0, 0, 0, 0)
    q_copy(1, 1).wait_recv()
    step0(0, True)

    def first_phase(k, _):
        @pl.when(k == 1)
        def _():
            q_copy(2, 0).wait_recv()
            q_copy(2, 1).wait_recv()
            q_copy(5, 1).start()

        @pl.when(k == 2)
        def _():
            ring_step(2, 0)
            for i in (3, 4):
                q_copy(i, 1).wait_recv()
                q_copy(i + 3, 1).start()
            q_copy(3, 0).wait_recv()

        @pl.when(k == 3)
        def _():
            q_copy(4, 0).wait_recv()

        @pl.when(k == 4)
        def _():
            ring_step(2, 1)

        for i in (4, 5, 6):
            @pl.when(k == i)
            def _():
                q_copy(i + 1, 0).wait_recv()
                q_copy(i + 1, 1).wait_recv()

        step0(k)
        return 0

    lax.fori_loop(1, NR, first_phase, 0)
    ring_step(3, 0)
    ring_step(3, 1)

    def page_copy(k):
        to = (me + k) % 64
        return remote(pg_out.at[to], pool.at[me], pg_s.at[k], pg_r.at[k], ctx=to)

    def page_start(k, _):
        page_copy(k).start()
        return 0

    lax.fori_loop(1, 64, page_start, 0)

    for t, half, way in ((2, 1, 0), (2, 0, 1), (3, 0, 0), (3, 1, 1)):
        ring(t, half, way).wait_recv()

    scores(1, 1, 0, 0)

    def second_phase(j, _):
        k = j % NR
        scores(1, k, 1, 1)
        attend(1, k, 0, 0)
        scores(1, (j + 1) % NR, 0, 0)
        attend(1, k, 1, 1)
        for i in range(1, NR):
            @pl.when(j == i)
            def _():
                o_copy(i).start()
                st_copy(i).start()

        return 0

    lax.fori_loop(1, NR + 1, second_phase, 0)

    def page_wait(k, _):
        source = (me + 64 - k) % 64
        to = (me + k) % 64
        remote(pg_out.at[to], pool.at[source], pg_s.at[k], pg_r.at[k], ctx=to).wait()
        return 0

    lax.fori_loop(1, 64, page_wait, 0)
    own_pages.wait()
    pool_rows = pool[...].reshape(POOL, HD)
    found = lax.dot_general(dq, pool_rows, NT, preferred_element_type=F32)
    at = lax.broadcasted_iota(jnp.int32, (128, POOL), 1)
    slot_at = (at // 32) % 2 * 64 + (at // 64) % 2 * 32 + at // 128
    spread = (lax.broadcasted_iota(jnp.int32, (128, POOL), 0) == slot_at).astype(BF16)
    mine = lax.dot_general(owned, spread, (((0,), (0,)), ((), ())), preferred_element_type=F32)
    at = lax.broadcasted_iota(jnp.int32, (1, POOL), 1)
    found = jnp.where((mine > 0.5) & (at % 4 == col_head * 2), found, NEG)
    pool_m, pool_l, pool_p = weigh(found)
    pool_o = jnp.dot(pool_p, pool_rows, preferred_element_type=F32)
    both = jnp.maximum(res_m, pool_m)
    res_a = jnp.exp2(res_m - both)
    pool_a = jnp.exp2(pool_m - both)
    dec = (res_o * res_a + pool_o * pool_a) / (res_l * res_a + pool_l * pool_a)
    for h in range(8):
        lhs[TOK : TOK + 16, h * HD : (h + 1) * HD] = dec[h * 16 : (h + 1) * 16, :].astype(BF16)

    for k in range(1, NR):
        o_copy(k).wait()
        st_copy(k).wait()
    lse = [stbuf[0]] + [strecv[k] for k in range(1, NR)]
    top = functools.reduce(jnp.maximum, lse)
    share = [jnp.exp2(a - top) for a in lse]
    whole = 1.0 / functools.reduce(jnp.add, share)
    share = [a * whole for a in share]
    for h in range(8):
        head, g = h // GROUP, h % GROUP
        cols = slice(g * TOK, (g + 1) * TOK)
        merged = obuf[0, head, :, cols].astype(F32) * share[0][h : h + 1]
        for k in range(1, NR):
            merged = merged + orecv[k, head, :, cols].astype(F32) * share[k][h : h + 1]
        lhs[:TOK, h * HD : (h + 1) * HD] = merged.T.astype(BF16)

    core = tp % 2
    side = tp // 2
    sibling = side * 2 + (1 - core)
    across = (1 - side) * 2 + core
    local[9].wait()

    def first_copy(c):
        if c == CHUNKS:
            return remote(pdec.at[:, 1 - core], rdec, t1_s.at[c], t1_r.at[c], tp=sibling)
        return remote(pbuf.at[c, :, 1 - core], rbuf.at[c], t1_s.at[c], t1_r.at[c], tp=sibling)

    def second_copy(c):
        if c == CHUNKS:
            return remote(sdec, tdec, t2_s.at[c], t2_r.at[c], tp=across)
        return remote(sbuf.at[c], tbuf.at[c], t2_s.at[c], t2_r.at[c], tp=across)

    def second(c):
        first_copy(c).wait_recv()
        if c == CHUNKS:
            sdec[...] = (
                pdec[1 - side, core].astype(F32) + rdec[1 - side].astype(F32)
            ).astype(BF16)
        else:
            sbuf[c] = (
                pbuf[c, 1 - side, core].astype(F32) + rbuf[c, 1 - side].astype(F32)
            ).astype(BF16)
        second_copy(c).start()

    dec_parts = []
    for c in range(CHUNKS):
        part = jnp.dot(lhs[...], wbuf[:, c * COLS : (c + 1) * COLS], preferred_element_type=F32)
        pbuf[c] = part[:TOK].astype(BF16).reshape(2, 2, TOK // 4, COLS)
        dec_parts.append(part[TOK:])
        first_copy(c).start()
        if c > 0:
            second(c - 1)
    for t in range(4):
        rows = jnp.concatenate([part[t * 4 : (t + 1) * 4] for part in dec_parts], axis=0)
        pdec[t // 2, t % 2] = rows.astype(BF16)
    first_copy(CHUNKS).start()
    second(CHUNKS - 1)
    second(CHUNKS)
    for c in range(CHUNKS):
        second_copy(c).wait_recv()
        out_ref[:, c * COLS : (c + 1) * COLS] = (
            pbuf[c, side, core].astype(F32) + rbuf[c, side].astype(F32) + tbuf[c].astype(F32)
        ).astype(BF16)
    second_copy(CHUNKS).wait_recv()
    rows = pdec[side, core].astype(F32) + rdec[side].astype(F32) + tdec[...].astype(F32)
    dout_ref[...] = jnp.concatenate(
        [rows[c * 4 : (c + 1) * 4] for c in range(CHUNKS)], axis=1
    ).astype(BF16)

    for t in range(4):
        for half in range(2):
            for way in range(2):
                if t < 3 or half == way:
                    ring(t, half, way).wait_send()
    for k in range(1, NR):
        for head in range(2):
            q_copy(k, head).wait_send()
    for c in range(CHUNKS + 1):
        first_copy(c).wait_send()
        second_copy(c).wait_send()


def body(
    span_q, cache_kv, span_kv, span_blocks, parked_pages, page_dest, page_req,
    decode_cache, decode_lengths, decode_q, decode_kv, out_weight,
):
    smem = pl.BlockSpec(memory_space=pltpu.SMEM)
    vmem = pl.BlockSpec(memory_space=pltpu.VMEM)
    hbm = pl.BlockSpec(memory_space=pl.ANY)
    dma = pltpu.SemaphoreType.DMA
    out, dout = pl.pallas_call(
        kernel,
        name="layer",
        out_shape=[
            jax.ShapeDtypeStruct((TOK // 4, CHUNKS * COLS), BF16),
            jax.ShapeDtypeStruct((4, CHUNKS * COLS), BF16),
        ],
        in_specs=[smem] * 2 + [hbm] * 10,
        out_specs=[vmem, vmem],
        scratch_shapes=[
            pltpu.VMEM((8 * TOK, HD), BF16),
            pltpu.VMEM((2, 4 * TOK, HD), BF16),
            pltpu.VMEM((32, 128), jnp.int32),
            pltpu.VMEM((32, 128), jnp.int32),
            pltpu.VMEM((128, HD), BF16),
            pltpu.VMEM((64, HD), BF16),
            pltpu.VMEM((64, 128), jnp.int32),
            pltpu.SMEM((64, 128), jnp.int32),
            pltpu.SMEM((NR * NZ,), F32),
            pltpu.VMEM((4, NZ, 2, HD, HD), BF16),
            pltpu.VMEM((NR, 2, QROWS, HD), BF16),
            pltpu.VMEM((2, MOST_KEYS, QROWS), F32),
            pltpu.VMEM((NR, 2, HD + 8, QROWS), F32),
            pltpu.VMEM((NR, 2, 8, QROWS), F32),
            pltpu.VMEM((NR, 2, HD, QROWS), BF16),
            pltpu.VMEM((NR, 2, HD, QROWS), BF16),
            pltpu.VMEM((NR, 8, TOK), F32),
            pltpu.VMEM((NR, 8, TOK), F32),
            pltpu.VMEM((64, PAGE_ROWS, HD), BF16),
            pltpu.VMEM((64, 2 * PAGE_ROWS, HD), BF16),
            pltpu.VMEM((64, 2 * PAGE_ROWS, HD), BF16),
            pltpu.VMEM((4 * 2048, HD), BF16),
            pltpu.VMEM((8 * HD, CHUNKS * COLS), BF16),
            pltpu.VMEM((TOK + 16, 8 * HD), BF16),
            pltpu.VMEM((CHUNKS, 2, 2, TOK // 4, COLS), BF16),
            pltpu.VMEM((CHUNKS, 2, TOK // 4, COLS), BF16),
            pltpu.VMEM((CHUNKS, TOK // 4, COLS), BF16),
            pltpu.VMEM((CHUNKS, TOK // 4, COLS), BF16),
            pltpu.VMEM((2, 2, 16, COLS), BF16),
            pltpu.VMEM((2, 16, COLS), BF16),
            pltpu.VMEM((16, COLS), BF16),
            pltpu.VMEM((16, COLS), BF16),
            dma((12,)),
            dma((2, 4, 2)), dma((2, 4, 2)),
            dma((NR, 2)), dma((NR, 2)),
            dma((NR,)), dma((NR,)),
            dma((NR,)), dma((NR,)),
            dma((64,)), dma((64,)),
            dma((CHUNKS + 1,)), dma((CHUNKS + 1,)),
            dma((CHUNKS + 1,)), dma((CHUNKS + 1,)),
        ],
        compiler_params=pltpu.CompilerParams(
            collective_id=0, has_side_effects=True, vmem_limit_bytes=56 << 20
        ),
    )(
        span_blocks, decode_lengths, span_q.reshape(8 * TOK, HD),
        cache_kv.reshape(4 * TOK, HD), span_kv.reshape(4 * TOK, HD),
        parked_pages.reshape(64, PAGE_ROWS, HD), page_dest.reshape(32, 128), page_req.reshape(32, 128),
        decode_cache.reshape(4 * 2048, HD), decode_q.reshape(128, HD), decode_kv.reshape(64, HD),
        out_weight.reshape(8 * HD, CHUNKS * COLS),
    )
    return out, dout.reshape(1, 4, CHUNKS * COLS)


def solution(mesh):
    return jax.shard_map(
        body,
        mesh=mesh,
        in_specs=(
            P("ctx", "tp", None),
            P("ctx", "tp", None, None),
            P("ctx", "tp", None, None),
            P(),
            P("ctx", None, "tp", None, None),
            P(),
            P(),
            P("ctx", None, "tp", None, None),
            P("ctx"),
            P("ctx", None, "tp", None),
            P("ctx", None, "tp", None, None),
            P("tp", None, None),
        ),
        out_specs=(P(("ctx", "tp"), None), P(("ctx", "tp"), None, None)),
        check_vma=False,
    )
```

```python
import functools

import jax
import jax.numpy as jnp
from jax import lax
from jax.experimental import pallas as pl
from jax.experimental.pallas import tpu as pltpu
from jax.sharding import PartitionSpec as P

NEG = -1e30
LOG2E = 1.4426950408889634
MESH = pl.DeviceIdType.MESH
BF16 = jnp.bfloat16
F32 = jnp.float32
NT = (((1,), (1,)), ((), ()))

NZ, NR = 8, 8
TOK = 128
HD = 128
GROUP = 4
QROWS = GROUP * TOK
PHASES = ((0, 1, 7), (2, 6, 3, 5, 4))
MOST_KEYS = 5 * 2 * TOK
DX = (0, 0, 1, 3, 2, 1, 3, 2)
DY = (0, 1, 0, 0, 0, 1, 1, 1)
MESSAGES = 14
COLS = 1024
CHUNKS = 4
PAGE_ROWS = 32
POOL = 4096


def remote(src, dst, send, recv, **device):
    return pltpu.make_async_remote_copy(
        src_ref=src, dst_ref=dst, send_sem=send, recv_sem=recv, device_id=device, device_id_type=MESH
    )


def fold8(x):
    return jnp.max(x.reshape(x.shape[0] // 8, 8, x.shape[1]), axis=0)


def kernel(
    blocks_ref, lens_ref, q_in, cache_in, span_in, pages_in, dest_in, req_in, dcache_in, dq_in, dkv_in, w_in,
    out_ref, dout_ref,
    q_raw, kv_raw, dest, req, dq_raw, dkv, page_ix, page_at, hide,
    kvbuf, qbuf, s_ref, acc, peaks, obuf, orecv, stbuf, strecv, mbuf, mst, pages, pg_out, pool, dcache, wbuf,
    lhs, pbuf, rbuf, sbuf, tbuf, pdec, rdec, sdec, tdec,
    lsem, kv_s, kv_r, q_s, q_r, o_s, o_r, st_s, st_r, pg_s, pg_r, t1_s, t1_r, t2_s, t2_r,
):
    me = lax.axis_index("ctx")
    tp = lax.axis_index("tp")
    z = me // NR
    rest = me % NR
    y = rest // 4
    x = rest % 4
    score_c = (HD ** -0.5) * LOG2E

    def plane(dx, dy):
        return z * NR + ((y + dy) % 2) * 4 + (x + dx) % 4

    barrier = pltpu.get_barrier_semaphore()

    def greet(k, _):
        pl.semaphore_signal(barrier, inc=1, device_id={"ctx": (me + k) % 64}, device_id_type=MESH)
        return 0

    lax.fori_loop(1, 64, greet, 0)
    for k in range(1, 4):
        pl.semaphore_signal(barrier, inc=1, device_id={"tp": (tp + k) % 4}, device_id_type=MESH)

    moves = [
        (q_in, q_raw), (cache_in, kv_raw.at[0]), (span_in, kv_raw.at[1]), (dest_in, dest), (req_in, req),
        (pages_in, pages), (dq_in, dq_raw), (dkv_in, dkv), (dcache_in, dcache), (w_in, wbuf),
    ]
    local = [pltpu.make_async_copy(src, dst, lsem.at[i]) for i, (src, dst) in enumerate(moves)]
    for copy in local:
        copy.start()

    for k in range(NR):
        q_pos = blocks_ref[plane(4 - DX[k], DY[k])]
        for d in range(NZ):
            k_pos = blocks_ref[((z + d) % NZ) * NR + rest]
            hide[k * NZ + d] = jnp.minimum(q_pos - k_pos, 0).astype(F32) * -NEG

    row = lax.broadcasted_iota(jnp.int32, (128, 128), 0)
    lane = lax.broadcasted_iota(jnp.int32, (128, 128), 1)
    by_head = (lane == (row % 16) * 8 + row // 16).astype(BF16)
    by_kind = (lane == (row % 32) * 4 + row // 32).astype(BF16)
    local[0].wait()
    for b in range(8):
        part = jnp.dot(by_head, q_raw[b * 128 : (b + 1) * 128, :], preferred_element_type=F32)
        for h in range(8):
            at = (h % GROUP) * TOK + b * 16
            qbuf[0, h // GROUP, at : at + 16, :] = part[h * 16 : (h + 1) * 16].astype(BF16)
    local[1].wait()
    local[2].wait()
    for half in range(2):
        parts = [
            jnp.dot(by_kind, kv_raw[half, b * 128 : (b + 1) * 128, :], preferred_element_type=F32)
            for b in range(4)
        ]
        for h in range(2):
            first = h * 64
            keys = jnp.concatenate([part[first : first + 32] for part in parts], axis=0)
            values = jnp.concatenate([part[first + 32 : first + 64] for part in parts], axis=0)
            kvbuf[h, 0, half] = keys.astype(BF16)
            kvbuf[2 + h, 0, half] = values.T.astype(BF16)

    local[3].wait()
    own_row = dest[pl.ds(me // 2, 1), :]
    slot_lane = lax.broadcasted_iota(jnp.int32, (64, 128), 1)
    hit = (own_row == lax.broadcasted_iota(jnp.int32, (64, 128), 0)) & (slot_lane // 64 == me % 2)
    first = jnp.min(jnp.where(hit, slot_lane % 64, 63), axis=1, keepdims=True)
    last = jnp.max(jnp.where(hit, slot_lane % 64, 0), axis=1, keepdims=True)
    page_ix[...] = jnp.where(slot_lane < 64, first, last)
    to_smem = pltpu.make_async_copy(page_ix, page_at, lsem.at[10])
    to_smem.start()

    local[4].wait()
    code_lane = lax.broadcasted_iota(jnp.int32, (32, 128), 1)
    code = (code_lane % 64) * 4 + req[...]
    owners = [None] * 4
    for odd in range(2):
        hit = (dest[...] == me) & (code_lane // 64 == odd)
        low = jnp.min(jnp.where(hit, code, 1 << 20), axis=1, keepdims=True)
        high = jnp.max(jnp.where(hit, code, -1), axis=1, keepdims=True)
        owners[odd] = jnp.where(high >= 0, low % 4, -1)
        owners[2 + odd] = jnp.where(high > low, high % 4, -1)
    owner = jnp.concatenate(owners, axis=0)
    owned = (owner == (lane // 4) % 4).astype(BF16)
    to_smem.wait()

    pl.semaphore_wait(barrier, 66)

    def q_copy(k, head):
        if k < 5:
            src, to = 0, plane(DX[k], DY[k])
        elif head == 0:
            src, to = 1, plane(DX[k], 0)
        else:
            src, to = k - 3, plane(0, 1)
        return remote(qbuf.at[src, head], qbuf.at[k, head], q_s.at[k, head], q_r.at[k, head], ctx=to)

    def ring(t, half, way):
        here = (-t) % NZ if way == 0 else t
        there = (-t - 1) % NZ if way == 0 else t + 1
        to = (z + 1) % NZ if way == 0 else (z + NZ - 1) % NZ
        return remote(
            kvbuf.at[:, here, half], kvbuf.at[:, there, half],
            kv_s.at[way, t, half], kv_r.at[way, t, half], ctx=to * NR + rest,
        )

    def ring_step(t, half):
        for way in range(2):
            if t < 3 or half == way:
                if t > 0:
                    ring(t - 1, half, way).wait_recv()
                ring(t, half, way).start()

    q_copy(1, 0).start()
    ring_step(0, 0)
    for k in (2, 3, 4):
        q_copy(k, 1).start()
    ring_step(0, 1)
    for k in (2, 3, 4):
        q_copy(k, 0).start()
    q_copy(1, 1).start()

    local[5].wait()

    def place(t, _):
        for i in range(2):
            pg_out[t, i * PAGE_ROWS : (i + 1) * PAGE_ROWS, :] = pages[page_at[t, i * 64]]
        return 0

    lax.fori_loop(0, 64, place, 0)
    own_pages = pltpu.make_async_copy(pg_out.at[me], pool.at[me], lsem.at[11])
    own_pages.start()

    ring_step(1, 0)

    local[6].wait()
    local[7].wait()
    local[8].wait()
    dq = jnp.dot(by_head, dq_raw[...], preferred_element_type=F32).astype(BF16)
    col_req = (lax.broadcasted_iota(jnp.int32, (128, 1), 0) // 4) % 4
    col_step = lax.broadcasted_iota(jnp.int32, (128, 1), 0) % 4
    col_head = lax.broadcasted_iota(jnp.int32, (128, 1), 0) // 64
    length = jnp.zeros((128, 1), jnp.int32)
    for r in range(4):
        length = jnp.where(col_req == r, lens_ref[r], length)

    def weigh(scores):
        m = jnp.max(scores, axis=1, keepdims=True)
        p = jnp.exp2(scores * score_c - m * score_c)
        total = jnp.sum(p, axis=1, keepdims=True)
        return m * score_c, total, pltpu.roll(p, 1, 1).astype(BF16)

    wide = jnp.concatenate([dcache[r * 2048 : (r + 1) * 2048, :] for r in range(4)], axis=1)
    zero = jnp.zeros((), BF16)
    dq_wide = jnp.concatenate([jnp.where(col_req == r, dq, zero) for r in range(4)], axis=1)
    res = lax.dot_general(dq_wide, wide, NT, preferred_element_type=F32)
    at = lax.broadcasted_iota(jnp.int32, (1, 2048), 1)
    res = jnp.where((at // 4 < length) & (at % 4 == col_head * 2), res, NEG)
    new = lax.dot_general(dq, dkv[...], NT, preferred_element_type=F32)
    at = lax.broadcasted_iota(jnp.int32, (1, 64), 1)
    new = jnp.where(
        (at // 16 == col_req) & ((at // 4) % 4 <= col_step) & (at % 4 == col_head * 2), new, NEG
    )
    new = jnp.concatenate([new, jnp.full((128, 64), NEG, F32)], axis=1)
    res_m, res_l, res_p = weigh(jnp.concatenate([res, new], axis=1))
    part = jnp.dot(res_p[:, :2048], wide, preferred_element_type=F32)
    res_o = jnp.dot(res_p[:, 2048:2112], dkv[...], preferred_element_type=F32)
    for r in range(4):
        res_o = res_o + jnp.where(col_req == r, part[:, r * HD : (r + 1) * HD], 0.0)

    q_copy(1, 0).wait_recv()
    for k in (5, 6, 7):
        q_copy(k, 0).start()
    ring_step(1, 1)

    def scores(phase, k, head, slot):
        keys = jnp.concatenate([kvbuf[head, d].reshape(2 * TOK, HD) for d in PHASES[phase]], axis=0)
        s_ref[slot, : len(PHASES[phase]) * 2 * TOK, :] = lax.dot_general(
            keys, qbuf[k, head], NT, preferred_element_type=F32
        )

    def attend(phase, k, head, slot, own=False):
        peak = None if phase == 0 else peaks[k, head]
        shifts = []
        for i, d in enumerate(PHASES[phase]):
            cached = slice(i * 2 * TOK, (i * 2 + 1) * TOK)
            fresh = slice((i * 2 + 1) * TOK, (i * 2 + 2) * TOK)
            shifts.append(hide[k * NZ + d])
            top = fold8(s_ref[slot, cached, :])
            peak = top if peak is None else jnp.maximum(peak, top)
            if own and d == 0:
                key_at = lax.broadcasted_iota(jnp.int32, (TOK, QROWS), 0)
                query_at = lax.broadcasted_iota(jnp.int32, (TOK, QROWS), 1) % TOK
                s_ref[slot, fresh, :] = jnp.where(key_at <= query_at, s_ref[slot, fresh, :], NEG)
            peak = jnp.maximum(peak, fold8(s_ref[slot, fresh, :]) + shifts[-1])
        m = jnp.max(peak, axis=0, keepdims=True) * score_c
        weights = []
        values = []
        for i, d in enumerate(PHASES[phase]):
            cached = slice(i * 2 * TOK, (i * 2 + 1) * TOK)
            fresh = slice((i * 2 + 1) * TOK, (i * 2 + 2) * TOK)
            weights.append(jnp.exp2(s_ref[slot, cached, :] * score_c - m).astype(BF16))
            weights.append(jnp.exp2(s_ref[slot, fresh, :] * score_c - (m - shifts[i])).astype(BF16))
            values.append(kvbuf[2 + head, d, 0])
            values.append(kvbuf[2 + head, d, 1])
        values = jnp.concatenate(values, axis=1)
        values = jnp.concatenate([values, jnp.ones((16, values.shape[1]), BF16)], axis=0)
        o = jnp.dot(values, jnp.concatenate(weights, axis=0), preferred_element_type=F32)[: HD + 8]
        if phase == 0:
            acc[k, head] = o
            peaks[k, head] = peak
            return
        before = jnp.max(peaks[k, head], axis=0, keepdims=True) * score_c
        o = o + acc[k, head] * jnp.exp2(before - m)
        total = o[HD : HD + 1]
        obuf[k, head] = (o[:HD] * (1.0 / total)).astype(BF16)
        lse = m + jnp.log2(total)
        rows = [lse[:, g * TOK : (g + 1) * TOK] for g in range(GROUP)]
        stbuf[k, head] = jnp.concatenate(rows + rows, axis=0)

    def messages(i):
        if i < 4:
            k = (1, 5, 6, 7)[i]
            src, stat, to = obuf.at[k, 1], stbuf.at[k, 1], plane(0, 1)
        elif i < 7:
            src, stat, to = mbuf.at[i - 4], mst.at[i - 4], plane(4 - DX[i - 2], 0)
        elif i < 13:
            src, stat, to = obuf.at[i - 5, 0], stbuf.at[i - 5, 0], plane(4 - DX[i - 5], 0)
        else:
            src, stat, to = mbuf.at[3], mst.at[3], plane(0, 1)
        return [
            remote(src, orecv.at[i], o_s.at[i], o_r.at[i], ctx=to),
            remote(stat, strecv.at[i], st_s.at[i], st_r.at[i], ctx=to),
        ]

    def depart(i):
        for copy in messages(i):
            copy.start()

    def arrive(i):
        for copy in messages(i):
            copy.wait_recv()

    def merge(parts):
        stats = [stat[...] for _, stat in parts]
        top = functools.reduce(jnp.maximum, stats)
        share = [jnp.exp2(a - top) for a in stats]
        whole = functools.reduce(jnp.add, share)
        scale = 1.0 / whole
        merged = None
        for (ref, _), a in zip(parts, share):
            a = a * scale
            wide = jnp.concatenate([a[g : g + 1] for g in range(GROUP)], axis=1)
            term = ref[...].astype(F32) * wide
            merged = term if merged is None else merged + term
        return merged, top + jnp.log2(whole)

    def mine_of(k, head):
        return obuf.at[k, head], stbuf.at[k, head]

    def came(i):
        return orecv.at[i], strecv.at[i]

    def relay(i, parts):
        merged, stat = merge(parts)
        mbuf[i] = merged.astype(BF16)
        mst[i] = stat

    def relay_head1(i):
        arrive(i - 3)
        relay(i - 4, [mine_of(i - 2, 1), came(i - 3)])
        depart(i)

    def step0(k, own=False):
        scores(0, k, 1, 1)
        attend(0, k, 0, 0, own)
        scores(0, (k + 1) % NR, 0, 0)
        attend(0, k, 1, 1, own)

    scores(0, 0, 0, 0)
    q_copy(1, 1).wait_recv()
    step0(0, True)

    def first_phase(k, _):
        @pl.when(k == 1)
        def _():
            q_copy(2, 0).wait_recv()
            q_copy(2, 1).wait_recv()
            q_copy(5, 1).start()

        @pl.when(k == 2)
        def _():
            ring_step(2, 0)
            for i in (3, 4):
                q_copy(i, 1).wait_recv()
                q_copy(i + 3, 1).start()
            q_copy(3, 0).wait_recv()

        @pl.when(k == 3)
        def _():
            q_copy(4, 0).wait_recv()

        @pl.when(k == 4)
        def _():
            ring_step(2, 1)

        for i in (4, 5, 6):
            @pl.when(k == i)
            def _():
                q_copy(i + 1, 0).wait_recv()
                q_copy(i + 1, 1).wait_recv()

        step0(k)
        return 0

    lax.fori_loop(1, NR, first_phase, 0)
    ring_step(3, 0)
    ring_step(3, 1)

    def page_copy(k):
        to = (me + k) % 64
        return remote(pg_out.at[to], pool.at[me], pg_s.at[k], pg_r.at[k], ctx=to)

    def page_start(k, _):
        page_copy(k).start()
        return 0

    lax.fori_loop(1, 64, page_start, 0)

    for t, half, way in ((2, 1, 0), (2, 0, 1), (3, 0, 0), (3, 1, 1)):
        ring(t, half, way).wait_recv()

    scores(1, 1, 0, 0)

    def second_at(j):
        t = (j + 1) // 3
        return (j + 3 * (t % 2) - 3 * (t // 2)) % NR

    def second_phase(j, _):
        k = second_at(j)
        scores(1, k, 1, 1)
        attend(1, k, 0, 0)
        scores(1, second_at(j + 1), 0, 0)
        attend(1, k, 1, 1)

        @pl.when(j == 1)
        def _():
            depart(0)

        for i in (2, 3, 4):
            @pl.when(j == i)
            def _():
                depart(i - 1)
                depart(i + 8)

        for i in (5, 6, 7):
            @pl.when(j == i)
            def _():
                depart(i + 2)

        for i in (6, 7):
            @pl.when(j == i)
            def _():
                relay_head1(i - 2)

        return 0

    lax.fori_loop(1, NR + 1, second_phase, 0)
    for i in (10, 11, 12):
        arrive(i)
    relay(3, [mine_of(1, 0), came(10), came(11), came(12)])
    depart(13)
    relay_head1(6)

    for head in range(2):
        others = (13, 7, 8, 9) if head == 0 else (0, 4, 5, 6)
        for i in others:
            arrive(i)
        merged, _ = merge([mine_of(0, head)] + [came(i) for i in others])
        for g in range(GROUP):
            h = head * GROUP + g
            lhs[:, h * HD : (h + 1) * HD] = merged[:, g * TOK : (g + 1) * TOK].T.astype(BF16)

    core = tp % 2
    side = tp // 2
    sibling = side * 2 + (1 - core)
    across = (1 - side) * 2 + core
    local[9].wait()

    def first_copy(c):
        if c == CHUNKS:
            return remote(pdec.at[:, 1 - core], rdec, t1_s.at[c], t1_r.at[c], tp=sibling)
        return remote(pbuf.at[c, :, 1 - core], rbuf.at[c], t1_s.at[c], t1_r.at[c], tp=sibling)

    def second_copy(c):
        if c == CHUNKS:
            return remote(sdec, tdec, t2_s.at[c], t2_r.at[c], tp=across)
        return remote(sbuf.at[c], tbuf.at[c], t2_s.at[c], t2_r.at[c], tp=across)

    def second(c):
        first_copy(c).wait_recv()
        if c == CHUNKS:
            sdec[...] = (
                pdec[1 - side, core].astype(F32) + rdec[1 - side].astype(F32)
            ).astype(BF16)
        else:
            sbuf[c] = (
                pbuf[c, 1 - side, core].astype(F32) + rbuf[c, 1 - side].astype(F32)
            ).astype(BF16)
        second_copy(c).start()

    for c in range(CHUNKS):
        part = jnp.dot(lhs[...], wbuf[:, c * COLS : (c + 1) * COLS], preferred_element_type=F32)
        pbuf[c] = part.astype(BF16).reshape(2, 2, TOK // 4, COLS)
        first_copy(c).start()
        if c > 0:
            second(c - 1)
    second(CHUNKS - 1)

    def page_wait(k, _):
        source = (me + 64 - k) % 64
        to = (me + k) % 64
        remote(pg_out.at[to], pool.at[source], pg_s.at[k], pg_r.at[k], ctx=to).wait()
        return 0

    lax.fori_loop(1, 64, page_wait, 0)
    own_pages.wait()
    pool_rows = pool[...].reshape(POOL, HD)
    found = lax.dot_general(dq, pool_rows, NT, preferred_element_type=F32)
    at = lax.broadcasted_iota(jnp.int32, (128, POOL), 1)
    slot_at = (at // 32) % 2 * 64 + (at // 64) % 2 * 32 + at // 128
    spread = (lax.broadcasted_iota(jnp.int32, (128, POOL), 0) == slot_at).astype(BF16)
    mine = lax.dot_general(owned, spread, (((0,), (0,)), ((), ())), preferred_element_type=F32)
    at = lax.broadcasted_iota(jnp.int32, (1, POOL), 1)
    found = jnp.where((mine > 0.5) & (at % 4 == col_head * 2), found, NEG)
    pool_m, pool_l, pool_p = weigh(found)
    pool_o = jnp.dot(pool_p, pool_rows, preferred_element_type=F32)
    both = jnp.maximum(res_m, pool_m)
    res_a = jnp.exp2(res_m - both)
    pool_a = jnp.exp2(pool_m - both)
    dec = (res_o * res_a + pool_o * pool_a) / (res_l * res_a + pool_l * pool_a)
    dec = jnp.concatenate([dec[h * 16 : (h + 1) * 16] for h in range(8)], axis=1).astype(BF16)
    dec_parts = [
        jnp.dot(dec, wbuf[:, c * COLS : (c + 1) * COLS], preferred_element_type=F32)
        for c in range(CHUNKS)
    ]
    for t in range(4):
        rows = jnp.concatenate([part[t * 4 : (t + 1) * 4] for part in dec_parts], axis=0)
        pdec[t // 2, t % 2] = rows.astype(BF16)
    first_copy(CHUNKS).start()
    for c in range(CHUNKS):
        second_copy(c).wait_recv()
        out_ref[:, c * COLS : (c + 1) * COLS] = (
            pbuf[c, side, core].astype(F32) + rbuf[c, side].astype(F32) + tbuf[c].astype(F32)
        ).astype(BF16)
        if c == 1:
            second(CHUNKS)
    second_copy(CHUNKS).wait_recv()
    rows = pdec[side, core].astype(F32) + rdec[side].astype(F32) + tdec[...].astype(F32)
    dout_ref[0] = jnp.concatenate(
        [rows[c * 4 : (c + 1) * 4] for c in range(CHUNKS)], axis=1
    ).astype(BF16)

    for t in range(4):
        for half in range(2):
            for way in range(2):
                if t < 3 or half == way:
                    ring(t, half, way).wait_send()
    for k in range(1, NR):
        for head in range(2):
            q_copy(k, head).wait_send()
    for i in range(MESSAGES):
        for copy in messages(i):
            copy.wait_send()
    for c in range(CHUNKS + 1):
        first_copy(c).wait_send()
        second_copy(c).wait_send()


def hand_out(out_in, dout_in, out_ref, dout_ref, sem):
    copies = [
        pltpu.make_async_copy(out_in, out_ref, sem.at[0]),
        pltpu.make_async_copy(dout_in, dout_ref, sem.at[1]),
    ]
    for copy in copies:
        copy.start()
    for copy in copies:
        copy.wait()


def body(
    span_q, cache_kv, span_kv, span_blocks, parked_pages, page_dest, page_req,
    decode_cache, decode_lengths, decode_q, decode_kv, out_weight,
):
    smem = pl.BlockSpec(memory_space=pltpu.SMEM)
    vmem = pl.BlockSpec(memory_space=pltpu.VMEM)
    hbm = pl.BlockSpec(memory_space=pl.ANY)
    dma = pltpu.SemaphoreType.DMA
    out, dout = pl.pallas_call(
        kernel,
        name="layer",
        out_shape=[
            jax.ShapeDtypeStruct((TOK // 4, CHUNKS * COLS), BF16),
            jax.ShapeDtypeStruct((1, 4, CHUNKS * COLS), BF16),
        ],
        in_specs=[smem] * 2 + [hbm] * 10,
        out_specs=[vmem, vmem],
        scratch_shapes=[
            pltpu.VMEM((8 * TOK, HD), BF16),
            pltpu.VMEM((2, 4 * TOK, HD), BF16),
            pltpu.VMEM((32, 128), jnp.int32),
            pltpu.VMEM((32, 128), jnp.int32),
            pltpu.VMEM((128, HD), BF16),
            pltpu.VMEM((64, HD), BF16),
            pltpu.VMEM((64, 128), jnp.int32),
            pltpu.SMEM((64, 128), jnp.int32),
            pltpu.SMEM((NR * NZ,), F32),
            pltpu.VMEM((4, NZ, 2, HD, HD), BF16),
            pltpu.VMEM((NR, 2, QROWS, HD), BF16),
            pltpu.VMEM((2, MOST_KEYS, QROWS), F32),
            pltpu.VMEM((NR, 2, HD + 8, QROWS), F32),
            pltpu.VMEM((NR, 2, 8, QROWS), F32),
            pltpu.VMEM((NR, 2, HD, QROWS), BF16),
            pltpu.VMEM((MESSAGES, HD, QROWS), BF16),
            pltpu.VMEM((NR, 2, 8, TOK), F32),
            pltpu.VMEM((MESSAGES, 8, TOK), F32),
            pltpu.VMEM((4, HD, QROWS), BF16),
            pltpu.VMEM((4, 8, TOK), F32),
            pltpu.VMEM((64, PAGE_ROWS, HD), BF16),
            pltpu.VMEM((64, 2 * PAGE_ROWS, HD), BF16),
            pltpu.VMEM((64, 2 * PAGE_ROWS, HD), BF16),
            pltpu.VMEM((4 * 2048, HD), BF16),
            pltpu.VMEM((8 * HD, CHUNKS * COLS), BF16),
            pltpu.VMEM((TOK, 8 * HD), BF16),
            pltpu.VMEM((CHUNKS, 2, 2, TOK // 4, COLS), BF16),
            pltpu.VMEM((CHUNKS, 2, TOK // 4, COLS), BF16),
            pltpu.VMEM((CHUNKS, TOK // 4, COLS), BF16),
            pltpu.VMEM((CHUNKS, TOK // 4, COLS), BF16),
            pltpu.VMEM((2, 2, 16, COLS), BF16),
            pltpu.VMEM((2, 16, COLS), BF16),
            pltpu.VMEM((16, COLS), BF16),
            pltpu.VMEM((16, COLS), BF16),
            dma((12,)),
            dma((2, 4, 2)), dma((2, 4, 2)),
            dma((NR, 2)), dma((NR, 2)),
            dma((MESSAGES,)), dma((MESSAGES,)),
            dma((MESSAGES,)), dma((MESSAGES,)),
            dma((64,)), dma((64,)),
            dma((CHUNKS + 1,)), dma((CHUNKS + 1,)),
            dma((CHUNKS + 1,)), dma((CHUNKS + 1,)),
        ],
        compiler_params=pltpu.CompilerParams(
            collective_id=0, has_side_effects=True, vmem_limit_bytes=56 << 20
        ),
    )(
        span_blocks, decode_lengths, span_q.reshape(8 * TOK, HD),
        cache_kv.reshape(4 * TOK, HD), span_kv.reshape(4 * TOK, HD),
        parked_pages.reshape(64, PAGE_ROWS, HD), page_dest.reshape(32, 128), page_req.reshape(32, 128),
        decode_cache.reshape(4 * 2048, HD), decode_q.reshape(128, HD), decode_kv.reshape(64, HD),
        out_weight.reshape(8 * HD, CHUNKS * COLS),
    )
    return pl.pallas_call(
        hand_out,
        name="results",
        out_shape=[jax.ShapeDtypeStruct(a.shape, a.dtype) for a in (out, dout)],
        in_specs=[hbm, hbm],
        out_specs=[hbm, hbm],
        scratch_shapes=[dma((2,))],
        compiler_params=pltpu.CompilerParams(vmem_limit_bytes=56 << 20),
    )(out, dout)


def solution(mesh):
    return jax.shard_map(
        body,
        mesh=mesh,
        in_specs=(
            P("ctx", "tp", None),
            P("ctx", "tp", None, None),
            P("ctx", "tp", None, None),
            P(),
            P("ctx", None, "tp", None, None),
            P(),
            P(),
            P("ctx", None, "tp", None, None),
            P("ctx"),
            P("ctx", None, "tp", None),
            P("ctx", None, "tp", None, None),
            P("tp", None, None),
        ),
        out_specs=(P(("ctx", "tp"), None), P(("ctx", "tp"), None, None)),
        check_vma=False,
    )
```

```python
import functools

import jax
import jax.numpy as jnp
from jax import lax
from jax.experimental import pallas as pl
from jax.experimental.pallas import tpu as pltpu
from jax.sharding import PartitionSpec as P

NEG = -1e30
LOG2E = 1.4426950408889634
MESH = pl.DeviceIdType.MESH
BF16 = jnp.bfloat16
F32 = jnp.float32
NT = (((1,), (1,)), ((), ()))

NZ, NR = 8, 8
TOK = 128
HD = 128
GROUP = 4
QROWS = GROUP * TOK
PHASES = ((0, 1, 7), (2, 6, 3, 5, 4))
MOST_KEYS = 5 * 2 * TOK
DX = (0, 0, 1, 3, 2, 1, 3, 2)
DY = (0, 1, 0, 0, 0, 1, 1, 1)
MESSAGES = 14
COLS = 1024
CHUNKS = 4
PAGE_ROWS = 32
POOL = 4096


def remote(src, dst, send, recv, **device):
    return pltpu.make_async_remote_copy(
        src_ref=src, dst_ref=dst, send_sem=send, recv_sem=recv, device_id=device, device_id_type=MESH
    )


def fold8(x):
    return jnp.max(x.reshape(x.shape[0] // 8, 8, x.shape[1]), axis=0)


def kernel(
    blocks_ref, lens_ref, q_in, cache_in, span_in, pages_in, dest_in, req_in, dcache_in, dq_in, dkv_in, w_in,
    out_ref, dout_ref,
    q_raw, kv_raw, dest, req, dq_raw, dkv, page_ix, page_at, hide,
    kvbuf, qbuf, s_ref, acc, peaks, obuf, orecv, stbuf, strecv, mbuf, mst, pages, pg_out, pool, pool_bias, dcache, wbuf,
    lhs, pbuf, rbuf, sbuf, tbuf, pdec, rdec, sdec, tdec,
    lsem, kv_s, kv_r, q_s, q_r, o_s, o_r, st_s, st_r, pg_s, pg_r, t1_s, t1_r, t2_s, t2_r,
):
    me = lax.axis_index("ctx")
    tp = lax.axis_index("tp")
    z = me // NR
    rest = me % NR
    y = rest // 4
    x = rest % 4
    score_c = (HD ** -0.5) * LOG2E

    def plane(dx, dy):
        return z * NR + ((y + dy) % 2) * 4 + (x + dx) % 4

    barrier = pltpu.get_barrier_semaphore()

    def greet(k, _):
        pl.semaphore_signal(barrier, inc=1, device_id={"ctx": (me + k) % 64}, device_id_type=MESH)
        return 0

    lax.fori_loop(1, 64, greet, 0)
    for k in range(1, 4):
        pl.semaphore_signal(barrier, inc=1, device_id={"tp": (tp + k) % 4}, device_id_type=MESH)

    moves = [
        (q_in, q_raw), (cache_in, kv_raw.at[0]), (span_in, kv_raw.at[1]), (dest_in, dest), (req_in, req),
        (pages_in, pages), (dq_in, dq_raw), (dkv_in, dkv), (dcache_in, dcache), (w_in, wbuf),
    ]
    local = [pltpu.make_async_copy(src, dst, lsem.at[i]) for i, (src, dst) in enumerate(moves)]
    for copy in local:
        copy.start()

    for k in range(NR):
        q_pos = blocks_ref[plane(4 - DX[k], DY[k])]
        for d in range(NZ):
            k_pos = blocks_ref[((z + d) % NZ) * NR + rest]
            hide[k * NZ + d] = jnp.minimum(q_pos - k_pos, 0).astype(F32) * -NEG

    row = lax.broadcasted_iota(jnp.int32, (128, 128), 0)
    lane = lax.broadcasted_iota(jnp.int32, (128, 128), 1)
    by_head = (lane == (row % 16) * 8 + row // 16).astype(BF16)
    by_kind = (lane == (row % 32) * 4 + row // 32).astype(BF16)
    local[0].wait()
    for b in range(8):
        part = jnp.dot(by_head, q_raw[b * 128 : (b + 1) * 128, :], preferred_element_type=F32)
        for h in range(8):
            at = (h % GROUP) * TOK + b * 16
            qbuf[0, h // GROUP, at : at + 16, :] = part[h * 16 : (h + 1) * 16].astype(BF16)
    local[1].wait()
    local[2].wait()
    for half in range(2):
        parts = [
            jnp.dot(by_kind, kv_raw[half, b * 128 : (b + 1) * 128, :], preferred_element_type=F32)
            for b in range(4)
        ]
        for h in range(2):
            first = h * 64
            keys = jnp.concatenate([part[first : first + 32] for part in parts], axis=0)
            values = jnp.concatenate([part[first + 32 : first + 64] for part in parts], axis=0)
            kvbuf[h, 0, half] = keys.astype(BF16)
            kvbuf[2 + h, 0, half] = values.T.astype(BF16)

    local[3].wait()
    own_row = dest[pl.ds(me // 2, 1), :]
    slot_lane = lax.broadcasted_iota(jnp.int32, (64, 128), 1)
    hit = (own_row == lax.broadcasted_iota(jnp.int32, (64, 128), 0)) & (slot_lane // 64 == me % 2)
    first = jnp.min(jnp.where(hit, slot_lane % 64, 63), axis=1, keepdims=True)
    last = jnp.max(jnp.where(hit, slot_lane % 64, 0), axis=1, keepdims=True)
    page_ix[...] = jnp.where(slot_lane < 64, first, last)
    to_smem = pltpu.make_async_copy(page_ix, page_at, lsem.at[10])
    to_smem.start()

    local[4].wait()
    code_lane = lax.broadcasted_iota(jnp.int32, (32, 128), 1)
    code = (code_lane % 64) * 4 + req[...]
    owners = [None] * 4
    for odd in range(2):
        hit = (dest[...] == me) & (code_lane // 64 == odd)
        low = jnp.min(jnp.where(hit, code, 1 << 20), axis=1, keepdims=True)
        high = jnp.max(jnp.where(hit, code, -1), axis=1, keepdims=True)
        owners[odd] = jnp.where(high >= 0, low % 4, -1)
        owners[2 + odd] = jnp.where(high > low, high % 4, -1)
    owner = jnp.concatenate(owners, axis=0)
    owned = (owner == (lane // 4) % 4).astype(BF16)
    to_smem.wait()

    pl.semaphore_wait(barrier, 66)

    def q_copy(k, head):
        if k < 5:
            src, to = 0, plane(DX[k], DY[k])
        elif head == 0:
            src, to = 1, plane(DX[k], 0)
        else:
            src, to = k - 3, plane(0, 1)
        return remote(qbuf.at[src, head], qbuf.at[k, head], q_s.at[k, head], q_r.at[k, head], ctx=to)

    def ring(t, half, way):
        here = (-t) % NZ if way == 0 else t
        there = (-t - 1) % NZ if way == 0 else t + 1
        to = (z + 1) % NZ if way == 0 else (z + NZ - 1) % NZ
        return remote(
            kvbuf.at[:, here, half], kvbuf.at[:, there, half],
            kv_s.at[way, t, half], kv_r.at[way, t, half], ctx=to * NR + rest,
        )

    def ring_step(t, half):
        for way in range(2):
            if t < 3 or half == way:
                if t > 0:
                    ring(t - 1, half, way).wait_recv()
                ring(t, half, way).start()

    q_copy(1, 0).start()
    ring_step(0, 0)
    for k in (2, 3, 4):
        q_copy(k, 1).start()
    ring_step(0, 1)
    for k in (2, 3, 4):
        q_copy(k, 0).start()
    q_copy(1, 1).start()

    local[5].wait()

    def place(t, _):
        for i in range(2):
            pg_out[t, i * PAGE_ROWS : (i + 1) * PAGE_ROWS, :] = pages[page_at[t, i * 64]]
        return 0

    lax.fori_loop(0, 64, place, 0)
    own_pages = pltpu.make_async_copy(pg_out.at[me], pool.at[me], lsem.at[11])
    own_pages.start()

    ring_step(1, 0)

    local[6].wait()
    local[7].wait()
    local[8].wait()
    dq = jnp.dot(by_head, dq_raw[...], preferred_element_type=F32).astype(BF16)
    col_req = (lax.broadcasted_iota(jnp.int32, (128, 1), 0) // 4) % 4
    col_step = lax.broadcasted_iota(jnp.int32, (128, 1), 0) % 4
    col_head = lax.broadcasted_iota(jnp.int32, (128, 1), 0) // 64
    length = jnp.zeros((128, 1), jnp.int32)
    for r in range(4):
        length = jnp.where(col_req == r, lens_ref[r], length)

    def weigh(scores):
        m = jnp.max(scores, axis=1, keepdims=True)
        p = jnp.exp2(scores * score_c - m * score_c)
        total = jnp.sum(p, axis=1, keepdims=True)
        return m * score_c, total, pltpu.roll(p, 1, 1).astype(BF16)

    wide = jnp.concatenate([dcache[r * 2048 : (r + 1) * 2048, :] for r in range(4)], axis=1)
    zero = jnp.zeros((), BF16)
    dq_wide = jnp.concatenate([jnp.where(col_req == r, dq, zero) for r in range(4)], axis=1)
    res = lax.dot_general(dq_wide, wide, NT, preferred_element_type=F32)
    at = lax.broadcasted_iota(jnp.int32, (1, 2048), 1)
    res = jnp.where((at // 4 < length) & (at % 4 == col_head * 2), res, NEG)
    new = lax.dot_general(dq, dkv[...], NT, preferred_element_type=F32)
    at = lax.broadcasted_iota(jnp.int32, (1, 64), 1)
    new = jnp.where(
        (at // 16 == col_req) & ((at // 4) % 4 <= col_step) & (at % 4 == col_head * 2), new, NEG
    )
    new = jnp.concatenate([new, jnp.full((128, 64), NEG, F32)], axis=1)
    res_m, res_l, res_p = weigh(jnp.concatenate([res, new], axis=1))
    part = jnp.dot(res_p[:, :2048], wide, preferred_element_type=F32)
    res_o = jnp.dot(res_p[:, 2048:2112], dkv[...], preferred_element_type=F32)
    for r in range(4):
        res_o = res_o + jnp.where(col_req == r, part[:, r * HD : (r + 1) * HD], 0.0)

    at = lax.broadcasted_iota(jnp.int32, (128, POOL), 1)
    slot_at = (at // 32) % 2 * 64 + (at // 64) % 2 * 32 + at // 128
    spread = (lax.broadcasted_iota(jnp.int32, (128, POOL), 0) == slot_at).astype(BF16)
    mine = lax.dot_general(owned, spread, (((0,), (0,)), ((), ())), preferred_element_type=F32)
    at = lax.broadcasted_iota(jnp.int32, (1, POOL), 1)
    pool_bias[...] = jnp.where((mine > 0.5) & (at % 4 == col_head * 2), 0.0, NEG)

    q_copy(1, 0).wait_recv()
    for k in (5, 6, 7):
        q_copy(k, 0).start()
    ring_step(1, 1)

    def scores(phase, k, head, slot):
        keys = jnp.concatenate([kvbuf[head, d].reshape(2 * TOK, HD) for d in PHASES[phase]], axis=0)
        s_ref[slot, : len(PHASES[phase]) * 2 * TOK, :] = lax.dot_general(
            keys, qbuf[k, head], NT, preferred_element_type=F32
        )

    def attend(phase, k, head, slot, own=False):
        peak = None if phase == 0 else peaks[k, head]
        shifts = []
        for i, d in enumerate(PHASES[phase]):
            cached = slice(i * 2 * TOK, (i * 2 + 1) * TOK)
            fresh = slice((i * 2 + 1) * TOK, (i * 2 + 2) * TOK)
            shifts.append(hide[k * NZ + d])
            top = fold8(s_ref[slot, cached, :])
            peak = top if peak is None else jnp.maximum(peak, top)
            if own and d == 0:
                key_at = lax.broadcasted_iota(jnp.int32, (TOK, QROWS), 0)
                query_at = lax.broadcasted_iota(jnp.int32, (TOK, QROWS), 1) % TOK
                s_ref[slot, fresh, :] = jnp.where(key_at <= query_at, s_ref[slot, fresh, :], NEG)
            peak = jnp.maximum(peak, fold8(s_ref[slot, fresh, :]) + shifts[-1])
        m = jnp.max(peak, axis=0, keepdims=True) * score_c
        weights = []
        values = []
        for i, d in enumerate(PHASES[phase]):
            cached = slice(i * 2 * TOK, (i * 2 + 1) * TOK)
            fresh = slice((i * 2 + 1) * TOK, (i * 2 + 2) * TOK)
            weights.append(jnp.exp2(s_ref[slot, cached, :] * score_c - m).astype(BF16))
            weights.append(jnp.exp2(s_ref[slot, fresh, :] * score_c - (m - shifts[i])).astype(BF16))
            values.append(kvbuf[2 + head, d, 0])
            values.append(kvbuf[2 + head, d, 1])
        values = jnp.concatenate(values, axis=1)
        values = jnp.concatenate([values, jnp.ones((16, values.shape[1]), BF16)], axis=0)
        o = jnp.dot(values, jnp.concatenate(weights, axis=0), preferred_element_type=F32)[: HD + 8]
        if phase == 0:
            acc[k, head] = o
            peaks[k, head] = peak
            return
        before = jnp.max(peaks[k, head], axis=0, keepdims=True) * score_c
        o = o + acc[k, head] * jnp.exp2(before - m)
        total = o[HD : HD + 1]
        obuf[k, head] = (o[:HD] * (1.0 / total)).astype(BF16)
        lse = m + jnp.log2(total)
        rows = [lse[:, g * TOK : (g + 1) * TOK] for g in range(GROUP)]
        stbuf[k, head] = jnp.concatenate(rows + rows, axis=0)

    def messages(i):
        if i < 4:
            k = (1, 5, 6, 7)[i]
            src, stat, to = obuf.at[k, 1], stbuf.at[k, 1], plane(0, 1)
        elif i < 7:
            src, stat, to = mbuf.at[i - 4], mst.at[i - 4], plane(4 - DX[i - 2], 0)
        elif i < 13:
            src, stat, to = obuf.at[i - 5, 0], stbuf.at[i - 5, 0], plane(4 - DX[i - 5], 0)
        else:
            src, stat, to = mbuf.at[3], mst.at[3], plane(0, 1)
        return [
            remote(src, orecv.at[i], o_s.at[i], o_r.at[i], ctx=to),
            remote(stat, strecv.at[i], st_s.at[i], st_r.at[i], ctx=to),
        ]

    def depart(i):
        for copy in messages(i):
            copy.start()

    def arrive(i):
        for copy in messages(i):
            copy.wait_recv()

    def merge(parts):
        stats = [stat[...] for _, stat in parts]
        top = functools.reduce(jnp.maximum, stats)
        share = [jnp.exp2(a - top) for a in stats]
        whole = functools.reduce(jnp.add, share)
        scale = 1.0 / whole
        merged = None
        for (ref, _), a in zip(parts, share):
            a = a * scale
            wide = jnp.concatenate([a[g : g + 1] for g in range(GROUP)], axis=1)
            term = ref[...].astype(F32) * wide
            merged = term if merged is None else merged + term
        return merged, top + jnp.log2(whole)

    def mine_of(k, head):
        return obuf.at[k, head], stbuf.at[k, head]

    def came(i):
        return orecv.at[i], strecv.at[i]

    def relay(i, parts):
        merged, stat = merge(parts)
        mbuf[i] = merged.astype(BF16)
        mst[i] = stat

    def relay_head1(i):
        arrive(i - 3)
        relay(i - 4, [mine_of(i - 2, 1), came(i - 3)])
        depart(i)

    def step0(k, own=False):
        scores(0, k, 1, 1)
        attend(0, k, 0, 0, own)
        scores(0, (k + 1) % NR, 0, 0)
        attend(0, k, 1, 1, own)

    scores(0, 0, 0, 0)
    q_copy(1, 1).wait_recv()
    step0(0, True)

    def first_phase(k, _):
        @pl.when(k == 1)
        def _():
            q_copy(2, 0).wait_recv()
            q_copy(2, 1).wait_recv()
            q_copy(5, 1).start()

        @pl.when(k == 2)
        def _():
            ring_step(2, 0)
            for i in (3, 4):
                q_copy(i, 1).wait_recv()
                q_copy(i + 3, 1).start()
            q_copy(3, 0).wait_recv()

        @pl.when(k == 3)
        def _():
            q_copy(4, 0).wait_recv()

        @pl.when(k == 4)
        def _():
            ring_step(2, 1)

        for i in (4, 5, 6):
            @pl.when(k == i)
            def _():
                q_copy(i + 1, 0).wait_recv()
                q_copy(i + 1, 1).wait_recv()

        step0(k)
        return 0

    lax.fori_loop(1, NR, first_phase, 0)
    ring_step(3, 0)
    ring_step(3, 1)

    def page_copy(k):
        to = (me + k) % 64
        return remote(pg_out.at[to], pool.at[me], pg_s.at[k], pg_r.at[k], ctx=to)

    def page_start(k, _):
        page_copy(k).start()
        return 0

    lax.fori_loop(1, 64, page_start, 0)

    for t, half, way in ((2, 1, 0), (2, 0, 1), (3, 0, 0), (3, 1, 1)):
        ring(t, half, way).wait_recv()

    scores(1, 1, 0, 0)

    def second_at(j):
        t = (j + 1) // 3
        return (j + 3 * (t % 2) - 3 * (t // 2)) % NR

    def second_phase(j, _):
        k = second_at(j)
        scores(1, k, 1, 1)
        attend(1, k, 0, 0)
        scores(1, second_at(j + 1), 0, 0)
        attend(1, k, 1, 1)

        @pl.when(j == 1)
        def _():
            depart(0)

        for i in (2, 3, 4):
            @pl.when(j == i)
            def _():
                depart(i - 1)
                depart(i + 8)

        for i in (5, 6, 7):
            @pl.when(j == i)
            def _():
                depart(i + 2)

        for i in (6, 7):
            @pl.when(j == i)
            def _():
                relay_head1(i - 2)

        return 0

    lax.fori_loop(1, NR + 1, second_phase, 0)
    for i in (10, 11, 12):
        arrive(i)
    relay(3, [mine_of(1, 0), came(10), came(11), came(12)])
    depart(13)
    relay_head1(6)

    for head in range(2):
        others = (13, 7, 8, 9) if head == 0 else (0, 4, 5, 6)
        for i in others:
            arrive(i)
        merged, _ = merge([mine_of(0, head)] + [came(i) for i in others])
        for g in range(GROUP):
            h = head * GROUP + g
            lhs[:, h * HD : (h + 1) * HD] = merged[:, g * TOK : (g + 1) * TOK].T.astype(BF16)

    core = tp % 2
    side = tp // 2
    sibling = side * 2 + (1 - core)
    across = (1 - side) * 2 + core
    local[9].wait()

    def first_copy(c):
        if c == CHUNKS:
            return remote(pdec.at[:, 1 - core], rdec, t1_s.at[c], t1_r.at[c], tp=sibling)
        return remote(pbuf.at[c, :, 1 - core], rbuf.at[c], t1_s.at[c], t1_r.at[c], tp=sibling)

    def second_copy(c):
        if c == CHUNKS:
            return remote(sdec, tdec, t2_s.at[c], t2_r.at[c], tp=across)
        return remote(sbuf.at[c], tbuf.at[c], t2_s.at[c], t2_r.at[c], tp=across)

    def second(c):
        first_copy(c).wait_recv()
        if c == CHUNKS:
            sdec[...] = (
                pdec[1 - side, core].astype(F32) + rdec[1 - side].astype(F32)
            ).astype(BF16)
        else:
            sbuf[c] = (
                pbuf[c, 1 - side, core].astype(F32) + rbuf[c, 1 - side].astype(F32)
            ).astype(BF16)
        second_copy(c).start()

    for c in range(CHUNKS):
        part = jnp.dot(lhs[...], wbuf[:, c * COLS : (c + 1) * COLS], preferred_element_type=F32)
        pbuf[c] = part.astype(BF16).reshape(2, 2, TOK // 4, COLS)
        first_copy(c).start()
        if c > 0:
            second(c - 1)
    second(CHUNKS - 1)

    def page_wait(k, _):
        source = (me + 64 - k) % 64
        to = (me + k) % 64
        remote(pg_out.at[to], pool.at[source], pg_s.at[k], pg_r.at[k], ctx=to).wait()
        return 0

    lax.fori_loop(1, 64, page_wait, 0)
    own_pages.wait()
    pool_rows = pool[...].reshape(POOL, HD)
    found = lax.dot_general(dq, pool_rows, NT, preferred_element_type=F32)
    found = found + pool_bias[...]
    pool_m, pool_l, pool_p = weigh(found)
    pool_o = jnp.dot(pool_p, pool_rows, preferred_element_type=F32)
    both = jnp.maximum(res_m, pool_m)
    res_a = jnp.exp2(res_m - both)
    pool_a = jnp.exp2(pool_m - both)
    dec = (res_o * res_a + pool_o * pool_a) / (res_l * res_a + pool_l * pool_a)
    dec = jnp.concatenate([dec[h * 16 : (h + 1) * 16] for h in range(8)], axis=1).astype(BF16)
    dec_parts = [
        jnp.dot(dec, wbuf[:, c * COLS : (c + 1) * COLS], preferred_element_type=F32)
        for c in range(CHUNKS)
    ]
    for t in range(4):
        rows = jnp.concatenate([part[t * 4 : (t + 1) * 4] for part in dec_parts], axis=0)
        pdec[t // 2, t % 2] = rows.astype(BF16)
    first_copy(CHUNKS).start()
    for c in range(CHUNKS):
        second_copy(c).wait_recv()
        out_ref[:, c * COLS : (c + 1) * COLS] = (
            pbuf[c, side, core].astype(F32) + rbuf[c, side].astype(F32) + tbuf[c].astype(F32)
        ).astype(BF16)
        if c == 1:
            second(CHUNKS)
    second_copy(CHUNKS).wait_recv()
    rows = pdec[side, core].astype(F32) + rdec[side].astype(F32) + tdec[...].astype(F32)
    dout_ref[0] = jnp.concatenate(
        [rows[c * 4 : (c + 1) * 4] for c in range(CHUNKS)], axis=1
    ).astype(BF16)

    for t in range(4):
        for half in range(2):
            for way in range(2):
                if t < 3 or half == way:
                    ring(t, half, way).wait_send()
    for k in range(1, NR):
        for head in range(2):
            q_copy(k, head).wait_send()
    for i in range(MESSAGES):
        for copy in messages(i):
            copy.wait_send()
    for c in range(CHUNKS + 1):
        first_copy(c).wait_send()
        second_copy(c).wait_send()


def hand_out(out_in, dout_in, out_ref, dout_ref):
    out_ref[...] = out_in[...]
    dout_ref[...] = dout_in[...]


def body(
    span_q, cache_kv, span_kv, span_blocks, parked_pages, page_dest, page_req,
    decode_cache, decode_lengths, decode_q, decode_kv, out_weight,
):
    smem = pl.BlockSpec(memory_space=pltpu.SMEM)
    vmem = pl.BlockSpec(memory_space=pltpu.VMEM)
    hbm = pl.BlockSpec(memory_space=pl.ANY)
    dma = pltpu.SemaphoreType.DMA
    out, dout = pl.pallas_call(
        kernel,
        name="layer",
        out_shape=[
            jax.ShapeDtypeStruct((TOK // 4, CHUNKS * COLS), BF16),
            jax.ShapeDtypeStruct((1, 4, CHUNKS * COLS), BF16),
        ],
        in_specs=[smem] * 2 + [hbm] * 10,
        out_specs=[vmem, vmem],
        scratch_shapes=[
            pltpu.VMEM((8 * TOK, HD), BF16),
            pltpu.VMEM((2, 4 * TOK, HD), BF16),
            pltpu.VMEM((32, 128), jnp.int32),
            pltpu.VMEM((32, 128), jnp.int32),
            pltpu.VMEM((128, HD), BF16),
            pltpu.VMEM((64, HD), BF16),
            pltpu.VMEM((64, 128), jnp.int32),
            pltpu.SMEM((64, 128), jnp.int32),
            pltpu.SMEM((NR * NZ,), F32),
            pltpu.VMEM((4, NZ, 2, HD, HD), BF16),
            pltpu.VMEM((NR, 2, QROWS, HD), BF16),
            pltpu.VMEM((2, MOST_KEYS, QROWS), F32),
            pltpu.VMEM((NR, 2, HD + 8, QROWS), F32),
            pltpu.VMEM((NR, 2, 8, QROWS), F32),
            pltpu.VMEM((NR, 2, HD, QROWS), BF16),
            pltpu.VMEM((MESSAGES, HD, QROWS), BF16),
            pltpu.VMEM((NR, 2, 8, TOK), F32),
            pltpu.VMEM((MESSAGES, 8, TOK), F32),
            pltpu.VMEM((4, HD, QROWS), BF16),
            pltpu.VMEM((4, 8, TOK), F32),
            pltpu.VMEM((64, PAGE_ROWS, HD), BF16),
            pltpu.VMEM((64, 2 * PAGE_ROWS, HD), BF16),
            pltpu.VMEM((64, 2 * PAGE_ROWS, HD), BF16),
            pltpu.VMEM((128, POOL), F32),
            pltpu.VMEM((4 * 2048, HD), BF16),
            pltpu.VMEM((8 * HD, CHUNKS * COLS), BF16),
            pltpu.VMEM((TOK, 8 * HD), BF16),
            pltpu.VMEM((CHUNKS, 2, 2, TOK // 4, COLS), BF16),
            pltpu.VMEM((CHUNKS, 2, TOK // 4, COLS), BF16),
            pltpu.VMEM((CHUNKS, TOK // 4, COLS), BF16),
            pltpu.VMEM((CHUNKS, TOK // 4, COLS), BF16),
            pltpu.VMEM((2, 2, 16, COLS), BF16),
            pltpu.VMEM((2, 16, COLS), BF16),
            pltpu.VMEM((16, COLS), BF16),
            pltpu.VMEM((16, COLS), BF16),
            dma((12,)),
            dma((2, 4, 2)), dma((2, 4, 2)),
            dma((NR, 2)), dma((NR, 2)),
            dma((MESSAGES,)), dma((MESSAGES,)),
            dma((MESSAGES,)), dma((MESSAGES,)),
            dma((64,)), dma((64,)),
            dma((CHUNKS + 1,)), dma((CHUNKS + 1,)),
            dma((CHUNKS + 1,)), dma((CHUNKS + 1,)),
        ],
        compiler_params=pltpu.CompilerParams(
            collective_id=0, has_side_effects=True, vmem_limit_bytes=56 << 20
        ),
    )(
        span_blocks, decode_lengths, span_q.reshape(8 * TOK, HD),
        cache_kv.reshape(4 * TOK, HD), span_kv.reshape(4 * TOK, HD),
        parked_pages.reshape(64, PAGE_ROWS, HD), page_dest.reshape(32, 128), page_req.reshape(32, 128),
        decode_cache.reshape(4 * 2048, HD), decode_q.reshape(128, HD), decode_kv.reshape(64, HD),
        out_weight.reshape(8 * HD, CHUNKS * COLS),
    )
    return pl.pallas_call(
        hand_out,
        name="results",
        out_shape=[jax.ShapeDtypeStruct(a.shape, a.dtype) for a in (out, dout)],
        in_specs=[vmem, vmem],
        out_specs=[vmem, vmem],
        compiler_params=pltpu.CompilerParams(vmem_limit_bytes=56 << 20),
    )(out, dout)


def solution(mesh):
    return jax.shard_map(
        body,
        mesh=mesh,
        in_specs=(
            P("ctx", "tp", None),
            P("ctx", "tp", None, None),
            P("ctx", "tp", None, None),
            P(),
            P("ctx", None, "tp", None, None),
            P(),
            P(),
            P("ctx", None, "tp", None, None),
            P("ctx"),
            P("ctx", None, "tp", None),
            P("ctx", None, "tp", None, None),
            P("tp", None, None),
        ),
        out_specs=(P(("ctx", "tp"), None), P(("ctx", "tp"), None, None)),
        check_vma=False,
    )
```

```python
import functools

import jax
import jax.numpy as jnp
from jax import lax
from jax.experimental import pallas as pl
from jax.experimental.pallas import tpu as pltpu
from jax.sharding import PartitionSpec as P

NEG = -1e30
LOG2E = 1.4426950408889634
MESH = pl.DeviceIdType.MESH
BF16 = jnp.bfloat16
F32 = jnp.float32
NT = (((1,), (1,)), ((), ()))

NZ, NR = 8, 8
TOK = 128
HD = 128
GROUP = 4
QROWS = GROUP * TOK
PHASES = ((0, 1, 7), (2, 6), (0, 1, 7, 2, 6), (3, 5, 4))
MOST_KEYS = 5 * 2 * TOK
DX = (0, 0, 1, 3, 2, 1, 3, 2)
DY = (0, 1, 0, 0, 0, 1, 1, 1)
MESSAGES = 14
PART = 16
POOL_EARLY = (0, 3)
POOL_LATE = (1, 2)
FIRST_HEAD = 0
COLS = 1024
CHUNKS = 4
PAGE_ROWS = 32
POOL = 4096


def remote(src, dst, send, recv, **device):
    return pltpu.make_async_remote_copy(
        src_ref=src, dst_ref=dst, send_sem=send, recv_sem=recv, device_id=device, device_id_type=MESH
    )


def fold8(x):
    return jnp.max(x.reshape(x.shape[0] // 8, 8, x.shape[1]), axis=0)


def kernel(
    blocks_ref, lens_ref, q_in, cache_in, span_in, pages_in, dest_in, req_in, dcache_in, dq_in, dkv_in, w_in,
    out_ref, dout_ref,
    q_raw, kv_raw, dest, req, dq_raw, dkv, page_ix, page_at, hide,
    kvbuf, qbuf, s_ref, acc, peaks, obuf, orecv, stbuf, strecv, mbuf, mst, pages, pg_out, pool, pool_bias, dcache, wbuf,
    lhs, pacc, pbuf, rbuf, sbuf, tbuf, pdec, rdec, sdec, tdec,
    lsem, kv_s, kv_r, q_s, q_r, o_s, o_r, st_s, st_r, pg_s, pg_r, t1_s, t1_r, t2_s, t2_r,
):
    me = lax.axis_index("ctx")
    tp = lax.axis_index("tp")
    z = me // NR
    rest = me % NR
    y = rest // 4
    x = rest % 4
    score_c = (HD ** -0.5) * LOG2E

    def plane(dx, dy):
        return z * NR + ((y + dy) % 2) * 4 + (x + dx) % 4

    barrier = pltpu.get_barrier_semaphore()

    def greet(k, _):
        pl.semaphore_signal(barrier, inc=1, device_id={"ctx": (me + k) % 64}, device_id_type=MESH)
        return 0

    lax.fori_loop(1, 64, greet, 0)
    for k in range(1, 4):
        pl.semaphore_signal(barrier, inc=1, device_id={"tp": (tp + k) % 4}, device_id_type=MESH)

    moves = [
        (q_in, q_raw), (cache_in, kv_raw.at[0]), (span_in, kv_raw.at[1]), (dest_in, dest), (req_in, req),
        (pages_in, pages), (dq_in, dq_raw), (dkv_in, dkv), (dcache_in, dcache), (w_in, wbuf),
    ]
    local = [pltpu.make_async_copy(src, dst, lsem.at[i]) for i, (src, dst) in enumerate(moves)]
    for copy in local:
        copy.start()

    for k in range(NR):
        q_pos = blocks_ref[plane(4 - DX[k], DY[k])]
        for d in range(NZ):
            k_pos = blocks_ref[((z + d) % NZ) * NR + rest]
            hide[k * NZ + d] = jnp.minimum(q_pos - k_pos, 0).astype(F32) * -NEG

    row = lax.broadcasted_iota(jnp.int32, (128, 128), 0)
    lane = lax.broadcasted_iota(jnp.int32, (128, 128), 1)
    by_head = (lane == (row % 16) * 8 + row // 16).astype(BF16)
    by_kind = (lane == (row % 32) * 4 + row // 32).astype(BF16)
    local[0].wait()
    for b in range(8):
        part = jnp.dot(by_head, q_raw[b * 128 : (b + 1) * 128, :], preferred_element_type=F32)
        for h in range(8):
            at = (h % GROUP) * TOK + b * 16
            qbuf[0, h // GROUP, at : at + 16, :] = part[h * 16 : (h + 1) * 16].astype(BF16)
    local[1].wait()
    local[2].wait()
    for half in range(2):
        parts = [
            jnp.dot(by_kind, kv_raw[half, b * 128 : (b + 1) * 128, :], preferred_element_type=F32)
            for b in range(4)
        ]
        for h in range(2):
            first = h * 64
            keys = jnp.concatenate([part[first : first + 32] for part in parts], axis=0)
            values = jnp.concatenate([part[first + 32 : first + 64] for part in parts], axis=0)
            kvbuf[h, 0, half] = keys.astype(BF16)
            kvbuf[2 + h, 0, half] = values.T.astype(BF16)

    local[3].wait()
    own_row = dest[pl.ds(me // 2, 1), :]
    slot_lane = lax.broadcasted_iota(jnp.int32, (64, 128), 1)
    hit = (own_row == lax.broadcasted_iota(jnp.int32, (64, 128), 0)) & (slot_lane // 64 == me % 2)
    first = jnp.min(jnp.where(hit, slot_lane % 64, 63), axis=1, keepdims=True)
    last = jnp.max(jnp.where(hit, slot_lane % 64, 0), axis=1, keepdims=True)
    page_ix[...] = jnp.where(slot_lane < 64, first, last)
    to_smem = pltpu.make_async_copy(page_ix, page_at, lsem.at[10])
    to_smem.start()

    local[4].wait()
    code_lane = lax.broadcasted_iota(jnp.int32, (32, 128), 1)
    code = (code_lane % 64) * 4 + req[...]
    owners = [None] * 4
    for odd in range(2):
        hit = (dest[...] == me) & (code_lane // 64 == odd)
        low = jnp.min(jnp.where(hit, code, 1 << 20), axis=1, keepdims=True)
        high = jnp.max(jnp.where(hit, code, -1), axis=1, keepdims=True)
        owners[odd] = jnp.where(high >= 0, low % 4, -1)
        owners[2 + odd] = jnp.where(high > low, high % 4, -1)
    owner = jnp.concatenate(owners, axis=0)
    owned = (owner == (lane // 4) % 4).astype(BF16)
    to_smem.wait()

    pl.semaphore_wait(barrier, 66)

    def q_copy(k, head):
        if k < 5:
            src, to = 0, plane(DX[k], DY[k])
        elif head == 0:
            src, to = 1, plane(DX[k], 0)
        else:
            src, to = k - 3, plane(0, 1)
        return remote(qbuf.at[src, head], qbuf.at[k, head], q_s.at[k, head], q_r.at[k, head], ctx=to)

    def ring(t, half, way):
        here = (-t) % NZ if way == 0 else t
        there = (-t - 1) % NZ if way == 0 else t + 1
        to = (z + 1) % NZ if way == 0 else (z + NZ - 1) % NZ
        return remote(
            kvbuf.at[:, here, half], kvbuf.at[:, there, half],
            kv_s.at[way, t, half], kv_r.at[way, t, half], ctx=to * NR + rest,
        )

    def ring_step(t, half):
        for way in range(2):
            if t < 3 or half == way:
                if t > 0:
                    ring(t - 1, half, way).wait_recv()
                ring(t, half, way).start()

    q_copy(1, 0).start()
    ring_step(0, 0)
    for k in (2, 3, 4):
        q_copy(k, 1).start()
    ring_step(0, 1)
    for k in (2, 3, 4):
        q_copy(k, 0).start()
    q_copy(1, 1).start()

    local[5].wait()

    def place(t, _):
        for i in range(2):
            pg_out[t, i * PAGE_ROWS : (i + 1) * PAGE_ROWS, :] = pages[page_at[t, i * 64]]
        return 0

    lax.fori_loop(0, 64, place, 0)
    own_pages = pltpu.make_async_copy(pg_out.at[me], pool.at[0], lsem.at[11])
    own_pages.start()

    ring_step(1, 0)

    local[6].wait()
    local[7].wait()
    local[8].wait()
    dq = jnp.dot(by_head, dq_raw[...], preferred_element_type=F32).astype(BF16)
    col_req = (lax.broadcasted_iota(jnp.int32, (128, 1), 0) // 4) % 4
    col_step = lax.broadcasted_iota(jnp.int32, (128, 1), 0) % 4
    col_head = lax.broadcasted_iota(jnp.int32, (128, 1), 0) // 64
    length = jnp.zeros((128, 1), jnp.int32)
    for r in range(4):
        length = jnp.where(col_req == r, lens_ref[r], length)

    def weigh(scores):
        m = jnp.max(scores, axis=1, keepdims=True)
        p = jnp.exp2(scores * score_c - m * score_c)
        total = jnp.sum(p, axis=1, keepdims=True)
        return m * score_c, total, pltpu.roll(p, 1, 1).astype(BF16)

    wide = jnp.concatenate([dcache[r * 2048 : (r + 1) * 2048, :] for r in range(4)], axis=1)
    zero = jnp.zeros((), BF16)
    dq_wide = jnp.concatenate([jnp.where(col_req == r, dq, zero) for r in range(4)], axis=1)
    res = lax.dot_general(dq_wide, wide, NT, preferred_element_type=F32)
    at = lax.broadcasted_iota(jnp.int32, (1, 2048), 1)
    res = jnp.where((at // 4 < length) & (at % 4 == col_head * 2), res, NEG)
    new = lax.dot_general(dq, dkv[...], NT, preferred_element_type=F32)
    at = lax.broadcasted_iota(jnp.int32, (1, 64), 1)
    new = jnp.where(
        (at // 16 == col_req) & ((at // 4) % 4 <= col_step) & (at % 4 == col_head * 2), new, NEG
    )
    new = jnp.concatenate([new, jnp.full((128, 64), NEG, F32)], axis=1)
    res_m, res_l, res_p = weigh(jnp.concatenate([res, new], axis=1))
    part = jnp.dot(res_p[:, :2048], wide, preferred_element_type=F32)
    res_o = jnp.dot(res_p[:, 2048:2112], dkv[...], preferred_element_type=F32)
    for r in range(4):
        res_o = res_o + jnp.where(col_req == r, part[:, r * HD : (r + 1) * HD], 0.0)

    at = lax.broadcasted_iota(jnp.int32, (128, POOL), 1)
    source = (me + 64 - at // 64) % 64
    slot_at = (at // 32) % 2 * 64 + source % 2 * 32 + source // 2
    spread = (lax.broadcasted_iota(jnp.int32, (128, POOL), 0) == slot_at).astype(BF16)
    mine = lax.dot_general(owned, spread, (((0,), (0,)), ((), ())), preferred_element_type=F32)
    at = lax.broadcasted_iota(jnp.int32, (1, POOL), 1)
    pool_bias[...] = jnp.where((mine > 0.5) & (at % 4 == col_head * 2), 0.0, NEG)

    q_copy(1, 0).wait_recv()
    for k in (5, 6, 7):
        q_copy(k, 0).start()
    ring_step(1, 1)

    def scores(phase, k, head, slot):
        keys = jnp.concatenate([kvbuf[head, d].reshape(2 * TOK, HD) for d in PHASES[phase]], axis=0)
        s_ref[slot, : len(PHASES[phase]) * 2 * TOK, :] = lax.dot_general(
            keys, qbuf[k, head], NT, preferred_element_type=F32
        )

    def attend(phase, k, head, slot, own=False):
        start = phase in (0, 2)
        peak = None if start else peaks[k, head]
        shifts = []
        for i, d in enumerate(PHASES[phase]):
            cached = slice(i * 2 * TOK, (i * 2 + 1) * TOK)
            fresh = slice((i * 2 + 1) * TOK, (i * 2 + 2) * TOK)
            shifts.append(hide[k * NZ + d])
            top = fold8(s_ref[slot, cached, :])
            peak = top if peak is None else jnp.maximum(peak, top)
            if own and d == 0:
                key_at = lax.broadcasted_iota(jnp.int32, (TOK, QROWS), 0)
                query_at = lax.broadcasted_iota(jnp.int32, (TOK, QROWS), 1) % TOK
                s_ref[slot, fresh, :] = jnp.where(key_at <= query_at, s_ref[slot, fresh, :], NEG)
            peak = jnp.maximum(peak, fold8(s_ref[slot, fresh, :]) + shifts[-1])
        m = jnp.max(peak, axis=0, keepdims=True) * score_c
        weights = []
        values = []
        for i, d in enumerate(PHASES[phase]):
            cached = slice(i * 2 * TOK, (i * 2 + 1) * TOK)
            fresh = slice((i * 2 + 1) * TOK, (i * 2 + 2) * TOK)
            weights.append(jnp.exp2(s_ref[slot, cached, :] * score_c - m).astype(BF16))
            weights.append(jnp.exp2(s_ref[slot, fresh, :] * score_c - (m - shifts[i])).astype(BF16))
            values.append(kvbuf[2 + head, d, 0])
            values.append(kvbuf[2 + head, d, 1])
        values = jnp.concatenate(values, axis=1)
        values = jnp.concatenate([values, jnp.ones((16, values.shape[1]), BF16)], axis=0)
        o = jnp.dot(values, jnp.concatenate(weights, axis=0), preferred_element_type=F32)[: HD + 8]
        if not start:
            before = jnp.max(peaks[k, head], axis=0, keepdims=True) * score_c
            o = o + acc[k, head] * jnp.exp2(before - m)
        if phase < 3:
            acc[k, head] = o
            peaks[k, head] = peak
            return
        total = o[HD : HD + 1]
        obuf[k, head] = (o[:HD] * (1.0 / total)).astype(BF16)
        lse = m + jnp.log2(total)
        rows = [lse[:, g * TOK : (g + 1) * TOK] for g in range(GROUP)]
        stbuf[k, head] = jnp.concatenate(rows + rows, axis=0)

    def messages(i):
        if i < 4:
            k = (1, 5, 6, 7)[i]
            src, stat, to = obuf.at[k, 1], stbuf.at[k, 1], plane(0, 1)
        elif i < 7:
            src, stat, to = mbuf.at[i - 4], mst.at[i - 4], plane(4 - DX[i - 2], 0)
        elif i < 13:
            src, stat, to = obuf.at[i - 5, 0], stbuf.at[i - 5, 0], plane(4 - DX[i - 5], 0)
        else:
            src, stat, to = mbuf.at[3], mst.at[3], plane(0, 1)
        return [
            remote(src, orecv.at[i], o_s.at[i], o_r.at[i], ctx=to),
            remote(stat, strecv.at[i], st_s.at[i], st_r.at[i], ctx=to),
        ]

    def depart(i):
        for copy in messages(i):
            copy.start()

    def arrive(i):
        for copy in messages(i):
            copy.wait_recv()

    def merge(parts):
        stats = [stat[...] for _, stat in parts]
        top = functools.reduce(jnp.maximum, stats)
        share = [jnp.exp2(a - top) for a in stats]
        whole = functools.reduce(jnp.add, share)
        scale = 1.0 / whole
        merged = None
        for (ref, _), a in zip(parts, share):
            a = a * scale
            wide = jnp.concatenate([a[g : g + 1] for g in range(GROUP)], axis=1)
            term = ref[...].astype(F32) * wide
            merged = term if merged is None else merged + term
        return merged, top + jnp.log2(whole)

    def mine_of(k, head):
        return obuf.at[k, head], stbuf.at[k, head]

    def came(i):
        return orecv.at[i], strecv.at[i]

    def relay(i, parts):
        merged, stat = merge(parts)
        mbuf[i] = merged.astype(BF16)
        mst[i] = stat

    def relay_head1(i):
        arrive(i - 3)
        relay(i - 4, [mine_of(i - 2, 1), came(i - 3)])
        depart(i)

    def step(phase, k, later, own=False):
        scores(phase, k, 1, 1)
        attend(phase, k, 0, 0, own)
        scores(phase, later, 0, 0)
        attend(phase, k, 1, 1, own)

    scores(0, 0, 0, 0)
    q_copy(1, 1).wait_recv()
    step(0, 0, 1, True)

    def first_phase(k, _):
        @pl.when(k == 1)
        def _():
            q_copy(2, 0).wait_recv()
            q_copy(2, 1).wait_recv()
            q_copy(5, 1).start()

        @pl.when(k == 2)
        def _():
            ring_step(2, 0)
            for i in (3, 4):
                q_copy(i, 1).wait_recv()
                q_copy(i + 3, 1).start()
            q_copy(3, 0).wait_recv()

        @pl.when(k == 3)
        def _():
            q_copy(4, 0).wait_recv()

        @pl.when(k == 4)
        def _():
            ring_step(2, 1)

        step(0, k, (k + 1) % 5)
        return 0

    lax.fori_loop(1, 5, first_phase, 0)
    scores(1, 0, 0, 0)

    def middle_phase(k, _):
        @pl.when(k == 2)
        def _():
            ring_step(3, 0)

        step(1, k, (k + 1) % 5)
        return 0

    lax.fori_loop(0, 5, middle_phase, 0)
    ring_step(3, 1)
    q_copy(5, 0).wait_recv()
    q_copy(5, 1).wait_recv()

    def page_copy(k):
        to = (me + k) % 64
        return remote(pg_out.at[to], pool.at[k], pg_s.at[k], pg_r.at[k], ctx=to)

    def page_start(k, _):
        page_copy(k).start()
        return 0

    lax.fori_loop(1, 64, page_start, 0)

    scores(2, 5, 0, 0)

    def late_phase(k, _):
        for i in (5, 6):
            @pl.when(k == i)
            def _():
                q_copy(i + 1, 0).wait_recv()
                q_copy(i + 1, 1).wait_recv()

        step(2, k, 5 + (k - 4) % 3)
        return 0

    lax.fori_loop(5, NR, late_phase, 0)
    for t, half, way in ((2, 1, 0), (2, 0, 1), (3, 0, 0), (3, 1, 1)):
        ring(t, half, way).wait_recv()

    scores(3, 1, 0, 0)

    def second_at(j):
        t = (j + 1) // 3
        return (j + 3 * (t % 2) - 3 * (t // 2)) % NR

    def second_phase(j, _):
        k = second_at(j)
        step(3, k, second_at(j + 1))

        @pl.when(j == 1)
        def _():
            depart(0)

        for i in (2, 3, 4):
            @pl.when(j == i)
            def _():
                depart(i - 1)
                depart(i + 8)

        for i in (5, 6, 7):
            @pl.when(j == i)
            def _():
                depart(i + 2)

        for i in (6, 7):
            @pl.when(j == i)
            def _():
                relay_head1(i - 2)

        return 0

    lax.fori_loop(1, NR + 1, second_phase, 0)
    for i in (10, 11, 12):
        arrive(i)
    relay(3, [mine_of(1, 0), came(10), came(11), came(12)])
    depart(13)
    relay_head1(6)

    def page_wait(k, _):
        page_copy(k).wait()
        return 0

    def pool_part(p, state):
        lax.fori_loop(max(1, p * PART), (p + 1) * PART, page_wait, 0)
        if p == 0:
            own_pages.wait()
        rows = pool[p * PART : (p + 1) * PART].reshape(PART * 64, HD)
        found = lax.dot_general(dq, rows, NT, preferred_element_type=F32)
        found = found + pool_bias[:, p * PART * 64 : (p + 1) * PART * 64]
        m, total, weights = weigh(found)
        o = jnp.dot(weights, rows, preferred_element_type=F32)
        both = jnp.maximum(state[0], m)
        old = jnp.exp2(state[0] - both)
        new = jnp.exp2(m - both)
        return both, state[1] * old + total * new, state[2] * old + o * new

    pool_state = (res_m, res_l, res_o)
    for p in POOL_EARLY:
        pool_state = pool_part(p, pool_state)

    def collect(head):
        others = (13, 7, 8, 9) if head == 0 else (0, 4, 5, 6)
        for i in others:
            arrive(i)
        merged, _ = merge([mine_of(0, head)] + [came(i) for i in others])
        for g in range(GROUP):
            lhs[head, :, g * HD : (g + 1) * HD] = merged[:, g * TOK : (g + 1) * TOK].T.astype(BF16)

    core = tp % 2
    side = tp // 2
    sibling = side * 2 + (1 - core)
    across = (1 - side) * 2 + core
    local[9].wait()
    half_width = GROUP * HD

    def first_copy(c):
        if c == CHUNKS:
            return remote(pdec.at[:, 1 - core], rdec, t1_s.at[c], t1_r.at[c], tp=sibling)
        return remote(pbuf.at[c, :, 1 - core], rbuf.at[c], t1_s.at[c], t1_r.at[c], tp=sibling)

    def second_copy(c):
        if c == CHUNKS:
            return remote(sdec, tdec, t2_s.at[c], t2_r.at[c], tp=across)
        return remote(sbuf.at[c], tbuf.at[c], t2_s.at[c], t2_r.at[c], tp=across)

    def second(c):
        first_copy(c).wait_recv()
        if c == CHUNKS:
            sdec[...] = (
                pdec[1 - side, core].astype(F32) + rdec[1 - side].astype(F32)
            ).astype(BF16)
        else:
            sbuf[c] = (
                pbuf[c, 1 - side, core].astype(F32) + rbuf[c, 1 - side].astype(F32)
            ).astype(BF16)
        second_copy(c).start()

    collect(FIRST_HEAD)
    for c in range(CHUNKS):
        weight = wbuf[FIRST_HEAD * half_width : (FIRST_HEAD + 1) * half_width, c * COLS : (c + 1) * COLS]
        pacc[c] = jnp.dot(lhs[FIRST_HEAD], weight, preferred_element_type=F32)
    last = 1 - FIRST_HEAD
    collect(last)
    for c in range(CHUNKS):
        weight = wbuf[last * half_width : (last + 1) * half_width, c * COLS : (c + 1) * COLS]
        part = pacc[c] + jnp.dot(lhs[last], weight, preferred_element_type=F32)
        pbuf[c] = part.astype(BF16).reshape(2, 2, TOK // 4, COLS)
        first_copy(c).start()
        if c > 0:
            second(c - 1)
    second(CHUNKS - 1)

    for p in POOL_LATE:
        pool_state = pool_part(p, pool_state)
    own_m, own_l, own_o = pool_state
    dec = own_o / own_l
    dec = jnp.concatenate([dec[h * 16 : (h + 1) * 16] for h in range(8)], axis=1).astype(BF16)
    dec_parts = [
        jnp.dot(dec, wbuf[:, c * COLS : (c + 1) * COLS], preferred_element_type=F32)
        for c in range(CHUNKS)
    ]
    for t in range(4):
        rows = jnp.concatenate([part[t * 4 : (t + 1) * 4] for part in dec_parts], axis=0)
        pdec[t // 2, t % 2] = rows.astype(BF16)
    first_copy(CHUNKS).start()
    for c in range(CHUNKS):
        second_copy(c).wait_recv()
        out_ref[:, c * COLS : (c + 1) * COLS] = (
            pbuf[c, side, core].astype(F32) + rbuf[c, side].astype(F32) + tbuf[c].astype(F32)
        ).astype(BF16)
        if c == 1:
            second(CHUNKS)
    second_copy(CHUNKS).wait_recv()
    rows = pdec[side, core].astype(F32) + rdec[side].astype(F32) + tdec[...].astype(F32)
    dout_ref[0] = jnp.concatenate(
        [rows[c * 4 : (c + 1) * 4] for c in range(CHUNKS)], axis=1
    ).astype(BF16)

    for t in range(4):
        for half in range(2):
            for way in range(2):
                if t < 3 or half == way:
                    ring(t, half, way).wait_send()
    for k in range(1, NR):
        for head in range(2):
            q_copy(k, head).wait_send()
    for i in range(MESSAGES):
        for copy in messages(i):
            copy.wait_send()
    for c in range(CHUNKS + 1):
        first_copy(c).wait_send()
        second_copy(c).wait_send()


def hand_out(out_in, dout_in, out_ref, dout_ref):
    out_ref[...] = out_in[...]
    dout_ref[...] = dout_in[...]


def body(
    span_q, cache_kv, span_kv, span_blocks, parked_pages, page_dest, page_req,
    decode_cache, decode_lengths, decode_q, decode_kv, out_weight,
):
    smem = pl.BlockSpec(memory_space=pltpu.SMEM)
    vmem = pl.BlockSpec(memory_space=pltpu.VMEM)
    hbm = pl.BlockSpec(memory_space=pl.ANY)
    dma = pltpu.SemaphoreType.DMA
    out, dout = pl.pallas_call(
        kernel,
        name="layer",
        out_shape=[
            jax.ShapeDtypeStruct((TOK // 4, CHUNKS * COLS), BF16),
            jax.ShapeDtypeStruct((1, 4, CHUNKS * COLS), BF16),
        ],
        in_specs=[smem] * 2 + [hbm] * 10,
        out_specs=[vmem, vmem],
        scratch_shapes=[
            pltpu.VMEM((8 * TOK, HD), BF16),
            pltpu.VMEM((2, 4 * TOK, HD), BF16),
            pltpu.VMEM((32, 128), jnp.int32),
            pltpu.VMEM((32, 128), jnp.int32),
            pltpu.VMEM((128, HD), BF16),
            pltpu.VMEM((64, HD), BF16),
            pltpu.VMEM((64, 128), jnp.int32),
            pltpu.SMEM((64, 128), jnp.int32),
            pltpu.SMEM((NR * NZ,), F32),
            pltpu.VMEM((4, NZ, 2, HD, HD), BF16),
            pltpu.VMEM((NR, 2, QROWS, HD), BF16),
            pltpu.VMEM((2, MOST_KEYS, QROWS), F32),
            pltpu.VMEM((NR, 2, HD + 8, QROWS), F32),
            pltpu.VMEM((NR, 2, 8, QROWS), F32),
            pltpu.VMEM((NR, 2, HD, QROWS), BF16),
            pltpu.VMEM((MESSAGES, HD, QROWS), BF16),
            pltpu.VMEM((NR, 2, 8, TOK), F32),
            pltpu.VMEM((MESSAGES, 8, TOK), F32),
            pltpu.VMEM((4, HD, QROWS), BF16),
            pltpu.VMEM((4, 8, TOK), F32),
            pltpu.VMEM((64, PAGE_ROWS, HD), BF16),
            pltpu.VMEM((64, 2 * PAGE_ROWS, HD), BF16),
            pltpu.VMEM((64, 2 * PAGE_ROWS, HD), BF16),
            pltpu.VMEM((128, POOL), F32),
            pltpu.VMEM((4 * 2048, HD), BF16),
            pltpu.VMEM((8 * HD, CHUNKS * COLS), BF16),
            pltpu.VMEM((2, TOK, GROUP * HD), BF16),
            pltpu.VMEM((CHUNKS, TOK, COLS), F32),
            pltpu.VMEM((CHUNKS, 2, 2, TOK // 4, COLS), BF16),
            pltpu.VMEM((CHUNKS, 2, TOK // 4, COLS), BF16),
            pltpu.VMEM((CHUNKS, TOK // 4, COLS), BF16),
            pltpu.VMEM((CHUNKS, TOK // 4, COLS), BF16),
            pltpu.VMEM((2, 2, 16, COLS), BF16),
            pltpu.VMEM((2, 16, COLS), BF16),
            pltpu.VMEM((16, COLS), BF16),
            pltpu.VMEM((16, COLS), BF16),
            dma((12,)),
            dma((2, 4, 2)), dma((2, 4, 2)),
            dma((NR, 2)), dma((NR, 2)),
            dma((MESSAGES,)), dma((MESSAGES,)),
            dma((MESSAGES,)), dma((MESSAGES,)),
            dma((64,)), dma((64,)),
            dma((CHUNKS + 1,)), dma((CHUNKS + 1,)),
            dma((CHUNKS + 1,)), dma((CHUNKS + 1,)),
        ],
        compiler_params=pltpu.CompilerParams(
            collective_id=0, has_side_effects=True, vmem_limit_bytes=56 << 20
        ),
    )(
        span_blocks, decode_lengths, span_q.reshape(8 * TOK, HD),
        cache_kv.reshape(4 * TOK, HD), span_kv.reshape(4 * TOK, HD),
        parked_pages.reshape(64, PAGE_ROWS, HD), page_dest.reshape(32, 128), page_req.reshape(32, 128),
        decode_cache.reshape(4 * 2048, HD), decode_q.reshape(128, HD), decode_kv.reshape(64, HD),
        out_weight.reshape(8 * HD, CHUNKS * COLS),
    )
    return pl.pallas_call(
        hand_out,
        name="results",
        out_shape=[jax.ShapeDtypeStruct(a.shape, a.dtype) for a in (out, dout)],
        in_specs=[vmem, vmem],
        out_specs=[vmem, vmem],
        compiler_params=pltpu.CompilerParams(vmem_limit_bytes=56 << 20),
    )(out, dout)


def solution(mesh):
    return jax.shard_map(
        body,
        mesh=mesh,
        in_specs=(
            P("ctx", "tp", None),
            P("ctx", "tp", None, None),
            P("ctx", "tp", None, None),
            P(),
            P("ctx", None, "tp", None, None),
            P(),
            P(),
            P("ctx", None, "tp", None, None),
            P("ctx"),
            P("ctx", None, "tp", None),
            P("ctx", None, "tp", None, None),
            P("tp", None, None),
        ),
        out_specs=(P(("ctx", "tp"), None), P(("ctx", "tp"), None, None)),
        check_vma=False,
    )
```

```python
import functools

import jax
import jax.numpy as jnp
from jax import lax
from jax.experimental import pallas as pl
from jax.experimental.pallas import tpu as pltpu
from jax.sharding import PartitionSpec as P

NEG = -1e30
LOG2E = 1.4426950408889634
MESH = pl.DeviceIdType.MESH
BF16 = jnp.bfloat16
F32 = jnp.float32
NT = (((1,), (1,)), ((), ()))

NZ, NR = 8, 8
TOK = 128
HD = 128
GROUP = 4
QROWS = GROUP * TOK
PHASES = ((0, 1, 7), (2, 6), (0, 1, 7, 2, 6), (3, 5, 4))
MOST_KEYS = 5 * 2 * TOK
DX = (0, 0, 1, 3, 2, 1, 3, 2)
DY = (0, 1, 0, 0, 0, 1, 1, 1)
MESSAGES = 14
PART = 16
POOL_EARLY = (0, 3)
POOL_LATE = (1, 2)
FIRST_HEAD = 0
COLS = 1024
CHUNKS = 4
PAGE_ROWS = 32
POOL = 4096


def remote(src, dst, send, recv, **device):
    return pltpu.make_async_remote_copy(
        src_ref=src, dst_ref=dst, send_sem=send, recv_sem=recv, device_id=device, device_id_type=MESH
    )


def fold8(x):
    return jnp.max(x.reshape(x.shape[0] // 8, 8, x.shape[1]), axis=0)


def kernel(
    blocks_ref, lens_ref, q_in, cache_in, span_in, pages_in, dest_in, req_in, dcache_in, dq_in, dkv_in, w_in,
    out_ref, dout_ref,
    q_raw, kv_raw, dest, req, dq_raw, dkv, page_ix, page_at, hide,
    kvbuf, qbuf, s_ref, acc, peaks, obuf, orecv, stbuf, strecv, mbuf, mst, pages, pg_out, pool, pool_bias, dcache, wbuf,
    lhs, pacc, pbuf, rbuf, sbuf, tbuf, pdec, rdec, sdec, tdec,
    lsem, kv_s, kv_r, q_s, q_r, o_s, o_r, st_s, st_r, pg_s, pg_r, t1_s, t1_r, t2_s, t2_r,
):
    me = lax.axis_index("ctx")
    tp = lax.axis_index("tp")
    z = me // NR
    rest = me % NR
    y = rest // 4
    x = rest % 4
    score_c = (HD ** -0.5) * LOG2E

    def plane(dx, dy):
        return z * NR + ((y + dy) % 2) * 4 + (x + dx) % 4

    barrier = pltpu.get_barrier_semaphore()

    def greet(k, _):
        pl.semaphore_signal(barrier, inc=1, device_id={"ctx": (me + k) % 64}, device_id_type=MESH)
        return 0

    lax.fori_loop(1, 64, greet, 0)
    for k in range(1, 4):
        pl.semaphore_signal(barrier, inc=1, device_id={"tp": (tp + k) % 4}, device_id_type=MESH)

    moves = [
        (q_in, q_raw), (cache_in, kv_raw.at[0]), (span_in, kv_raw.at[1]), (dest_in, dest), (req_in, req),
        (pages_in, pages), (dq_in, dq_raw), (dkv_in, dkv), (dcache_in, dcache), (w_in, wbuf),
    ]
    local = [pltpu.make_async_copy(src, dst, lsem.at[i]) for i, (src, dst) in enumerate(moves)]
    for copy in local:
        copy.start()

    for k in range(NR):
        q_pos = blocks_ref[plane(4 - DX[k], DY[k])]
        for d in range(NZ):
            k_pos = blocks_ref[((z + d) % NZ) * NR + rest]
            hide[k * NZ + d] = jnp.minimum(q_pos - k_pos, 0).astype(F32) * -NEG

    row = lax.broadcasted_iota(jnp.int32, (128, 128), 0)
    lane = lax.broadcasted_iota(jnp.int32, (128, 128), 1)
    by_head = (lane == (row % 16) * 8 + row // 16).astype(BF16)
    by_kind = (lane == (row % 32) * 4 + row // 32).astype(BF16)
    local[0].wait()
    for b in range(8):
        part = jnp.dot(by_head, q_raw[b * 128 : (b + 1) * 128, :], preferred_element_type=F32)
        for h in range(8):
            at = (h % GROUP) * TOK + b * 16
            qbuf[0, h // GROUP, at : at + 16, :] = part[h * 16 : (h + 1) * 16].astype(BF16)
    local[1].wait()
    local[2].wait()
    for half in range(2):
        parts = [
            jnp.dot(by_kind, kv_raw[half, b * 128 : (b + 1) * 128, :], preferred_element_type=F32)
            for b in range(4)
        ]
        for h in range(2):
            first = h * 64
            keys = jnp.concatenate([part[first : first + 32] for part in parts], axis=0)
            values = jnp.concatenate([part[first + 32 : first + 64] for part in parts], axis=0)
            kvbuf[h, 0, half] = keys.astype(BF16)
            kvbuf[2 + h, 0, half] = values.T.astype(BF16)

    local[3].wait()
    own_row = dest[pl.ds(me // 2, 1), :]
    slot_lane = lax.broadcasted_iota(jnp.int32, (64, 128), 1)
    hit = (own_row == lax.broadcasted_iota(jnp.int32, (64, 128), 0)) & (slot_lane // 64 == me % 2)
    first = jnp.min(jnp.where(hit, slot_lane % 64, 63), axis=1, keepdims=True)
    last = jnp.max(jnp.where(hit, slot_lane % 64, 0), axis=1, keepdims=True)
    page_ix[...] = jnp.where(slot_lane < 64, first, last)
    to_smem = pltpu.make_async_copy(page_ix, page_at, lsem.at[10])
    to_smem.start()

    local[4].wait()
    code_lane = lax.broadcasted_iota(jnp.int32, (32, 128), 1)
    code = (code_lane % 64) * 4 + req[...]
    owners = [None] * 4
    for odd in range(2):
        hit = (dest[...] == me) & (code_lane // 64 == odd)
        low = jnp.min(jnp.where(hit, code, 1 << 20), axis=1, keepdims=True)
        high = jnp.max(jnp.where(hit, code, -1), axis=1, keepdims=True)
        owners[odd] = jnp.where(high >= 0, low % 4, -1)
        owners[2 + odd] = jnp.where(high > low, high % 4, -1)
    owner = jnp.concatenate(owners, axis=0)
    owned = (owner == (lane // 4) % 4).astype(BF16)
    to_smem.wait()

    pl.semaphore_wait(barrier, 66)

    def q_copy(k, head):
        if k < 5:
            src, to = 0, plane(DX[k], DY[k])
        elif head == 0:
            src, to = 1, plane(DX[k], 0)
        else:
            src, to = k - 3, plane(0, 1)
        return remote(qbuf.at[src, head], qbuf.at[k, head], q_s.at[k, head], q_r.at[k, head], ctx=to)

    def ring(t, half, way):
        here = (-t) % NZ if way == 0 else t
        there = (-t - 1) % NZ if way == 0 else t + 1
        to = (z + 1) % NZ if way == 0 else (z + NZ - 1) % NZ
        return remote(
            kvbuf.at[:, here, half], kvbuf.at[:, there, half],
            kv_s.at[way, t, half], kv_r.at[way, t, half], ctx=to * NR + rest,
        )

    def ring_step(t, half):
        for way in range(2):
            if t < 3 or half == way:
                if t > 0:
                    ring(t - 1, half, way).wait_recv()
                ring(t, half, way).start()

    q_copy(1, 0).start()
    ring_step(0, 0)
    for k in (2, 3, 4):
        q_copy(k, 1).start()
    ring_step(0, 1)
    for k in (2, 3, 4):
        q_copy(k, 0).start()
    q_copy(1, 1).start()

    local[5].wait()

    def place(t, _):
        for i in range(2):
            pg_out[t, i * PAGE_ROWS : (i + 1) * PAGE_ROWS, :] = pages[page_at[t, i * 64]]
        return 0

    lax.fori_loop(0, 64, place, 0)
    own_pages = pltpu.make_async_copy(pg_out.at[me], pool.at[0], lsem.at[11])
    own_pages.start()

    ring_step(1, 0)

    local[6].wait()
    local[7].wait()
    local[8].wait()
    dq = jnp.dot(by_head, dq_raw[...], preferred_element_type=F32).astype(BF16)
    col_req = (lax.broadcasted_iota(jnp.int32, (128, 1), 0) // 4) % 4
    col_step = lax.broadcasted_iota(jnp.int32, (128, 1), 0) % 4
    col_head = lax.broadcasted_iota(jnp.int32, (128, 1), 0) // 64
    length = jnp.zeros((128, 1), jnp.int32)
    for r in range(4):
        length = jnp.where(col_req == r, lens_ref[r], length)

    def weigh(scores):
        m = jnp.max(scores, axis=1, keepdims=True)
        p = jnp.exp2(scores * score_c - m * score_c)
        total = jnp.sum(p, axis=1, keepdims=True)
        return m * score_c, total, pltpu.roll(p, 1, 1).astype(BF16)

    wide = jnp.concatenate([dcache[r * 2048 : (r + 1) * 2048, :] for r in range(4)], axis=1)
    zero = jnp.zeros((), BF16)
    dq_wide = jnp.concatenate([jnp.where(col_req == r, dq, zero) for r in range(4)], axis=1)
    res = lax.dot_general(dq_wide, wide, NT, preferred_element_type=F32)
    at = lax.broadcasted_iota(jnp.int32, (1, 2048), 1)
    res = jnp.where((at // 4 < length) & (at % 4 == col_head * 2), res, NEG)
    new = lax.dot_general(dq, dkv[...], NT, preferred_element_type=F32)
    at = lax.broadcasted_iota(jnp.int32, (1, 64), 1)
    new = jnp.where(
        (at // 16 == col_req) & ((at // 4) % 4 <= col_step) & (at % 4 == col_head * 2), new, NEG
    )
    new = jnp.concatenate([new, jnp.full((128, 64), NEG, F32)], axis=1)
    res_m, res_l, res_p = weigh(jnp.concatenate([res, new], axis=1))
    part = jnp.dot(res_p[:, :2048], wide, preferred_element_type=F32)
    res_o = jnp.dot(res_p[:, 2048:2112], dkv[...], preferred_element_type=F32)
    for r in range(4):
        res_o = res_o + jnp.where(col_req == r, part[:, r * HD : (r + 1) * HD], 0.0)

    at = lax.broadcasted_iota(jnp.int32, (128, POOL), 1)
    source = (me + 64 - at // 64) % 64
    slot_at = (at // 32) % 2 * 64 + source % 2 * 32 + source // 2
    spread = (lax.broadcasted_iota(jnp.int32, (128, POOL), 0) == slot_at).astype(BF16)
    mine = lax.dot_general(owned, spread, (((0,), (0,)), ((), ())), preferred_element_type=F32)
    at = lax.broadcasted_iota(jnp.int32, (1, POOL), 1)
    pool_bias[...] = jnp.where((mine > 0.5) & (at % 4 == col_head * 2), 0.0, NEG)

    q_copy(1, 0).wait_recv()
    for k in (5, 6, 7):
        q_copy(k, 0).start()
    ring_step(1, 1)

    def scores(phase, k, head, slot):
        keys = jnp.concatenate([kvbuf[head, d].reshape(2 * TOK, HD) for d in PHASES[phase]], axis=0)
        s_ref[slot, : len(PHASES[phase]) * 2 * TOK, :] = lax.dot_general(
            keys, qbuf[k, head], NT, preferred_element_type=F32
        )

    def attend(phase, k, head, slot, own=False):
        start = phase in (0, 2)
        peak = None if start else peaks[k, head]
        shifts = []
        for i, d in enumerate(PHASES[phase]):
            cached = slice(i * 2 * TOK, (i * 2 + 1) * TOK)
            fresh = slice((i * 2 + 1) * TOK, (i * 2 + 2) * TOK)
            shifts.append(hide[k * NZ + d])
            top = fold8(s_ref[slot, cached, :])
            peak = top if peak is None else jnp.maximum(peak, top)
            if own and d == 0:
                key_at = lax.broadcasted_iota(jnp.int32, (TOK, QROWS), 0)
                query_at = lax.broadcasted_iota(jnp.int32, (TOK, QROWS), 1) % TOK
                s_ref[slot, fresh, :] = jnp.where(key_at <= query_at, s_ref[slot, fresh, :], NEG)
            peak = jnp.maximum(peak, fold8(s_ref[slot, fresh, :]) + shifts[-1])
        m = jnp.max(peak, axis=0, keepdims=True) * score_c
        weights = []
        values = []
        for i, d in enumerate(PHASES[phase]):
            cached = slice(i * 2 * TOK, (i * 2 + 1) * TOK)
            fresh = slice((i * 2 + 1) * TOK, (i * 2 + 2) * TOK)
            weights.append(jnp.exp2(s_ref[slot, cached, :] * score_c - m).astype(BF16))
            weights.append(jnp.exp2(s_ref[slot, fresh, :] * score_c - (m - shifts[i])).astype(BF16))
            values.append(kvbuf[2 + head, d, 0])
            values.append(kvbuf[2 + head, d, 1])
        values = jnp.concatenate(values, axis=1)
        values = jnp.concatenate([values, jnp.ones((16, values.shape[1]), BF16)], axis=0)
        o = jnp.dot(values, jnp.concatenate(weights, axis=0), preferred_element_type=F32)[: HD + 8]
        if not start:
            before = jnp.max(peaks[k, head], axis=0, keepdims=True) * score_c
            o = o + acc[k, head] * jnp.exp2(before - m)
        if phase < 3:
            acc[k, head] = o
            peaks[k, head] = peak
            return
        total = o[HD : HD + 1]
        obuf[k, head] = (o[:HD] * (1.0 / total)).astype(BF16)
        lse = m + jnp.log2(total)
        rows = [lse[:, g * TOK : (g + 1) * TOK] for g in range(GROUP)]
        stbuf[k, head] = jnp.concatenate(rows + rows, axis=0)

    def messages(i):
        if i < 4:
            k = (1, 5, 6, 7)[i]
            src, stat, to = obuf.at[k, 1], stbuf.at[k, 1], plane(0, 1)
        elif i < 7:
            src, stat, to = mbuf.at[i - 4], mst.at[i - 4], plane(4 - DX[i - 2], 0)
        elif i < 13:
            src, stat, to = obuf.at[i - 5, 0], stbuf.at[i - 5, 0], plane(4 - DX[i - 5], 0)
        else:
            src, stat, to = mbuf.at[3], mst.at[3], plane(0, 1)
        return [
            remote(src, orecv.at[i], o_s.at[i], o_r.at[i], ctx=to),
            remote(stat, strecv.at[i], st_s.at[i], st_r.at[i], ctx=to),
        ]

    def depart(i):
        for copy in messages(i):
            copy.start()

    def arrive(i):
        for copy in messages(i):
            copy.wait_recv()

    def merge(parts):
        stats = [stat[...] for _, stat in parts]
        top = functools.reduce(jnp.maximum, stats)
        share = [jnp.exp2(a - top) for a in stats]
        whole = functools.reduce(jnp.add, share)
        scale = 1.0 / whole
        merged = None
        for (ref, _), a in zip(parts, share):
            a = a * scale
            wide = jnp.concatenate([a[g : g + 1] for g in range(GROUP)], axis=1)
            term = ref[...].astype(F32) * wide
            merged = term if merged is None else merged + term
        return merged, top + jnp.log2(whole)

    def mine_of(k, head):
        return obuf.at[k, head], stbuf.at[k, head]

    def came(i):
        return orecv.at[i], strecv.at[i]

    def relay(i, parts):
        merged, stat = merge(parts)
        mbuf[i] = merged.astype(BF16)
        mst[i] = stat

    def relay_head1(i):
        arrive(i - 3)
        relay(i - 4, [mine_of(i - 2, 1), came(i - 3)])
        depart(i)

    def step(phase, k, later, own=False):
        scores(phase, k, 1, 1)
        attend(phase, k, 0, 0, own)
        scores(phase, later, 0, 0)
        attend(phase, k, 1, 1, own)

    scores(0, 0, 0, 0)
    q_copy(1, 1).wait_recv()
    step(0, 0, 1, True)

    def first_phase(k, _):
        @pl.when(k == 1)
        def _():
            q_copy(2, 0).wait_recv()
            q_copy(2, 1).wait_recv()
            q_copy(5, 1).start()

        @pl.when(k == 2)
        def _():
            ring_step(2, 0)
            for i in (3, 4):
                q_copy(i, 1).wait_recv()
                q_copy(i + 3, 1).start()
            q_copy(3, 0).wait_recv()

        @pl.when(k == 3)
        def _():
            q_copy(4, 0).wait_recv()

        @pl.when(k == 4)
        def _():
            ring_step(2, 1)

        step(0, k, (k + 1) % 5)
        return 0

    lax.fori_loop(1, 5, first_phase, 0)
    scores(1, 0, 0, 0)

    def middle_phase(k, _):
        @pl.when(k == 2)
        def _():
            ring_step(3, 0)

        step(1, k, (k + 1) % 5)
        return 0

    lax.fori_loop(0, 5, middle_phase, 0)
    ring_step(3, 1)
    q_copy(5, 0).wait_recv()
    q_copy(5, 1).wait_recv()

    def page_copy(k):
        to = (me + k) % 64
        return remote(pg_out.at[to], pool.at[k], pg_s.at[k], pg_r.at[k], ctx=to)

    def page_start(k, _):
        page_copy(k).start()
        return 0

    lax.fori_loop(1, 64, page_start, 0)

    scores(2, 5, 0, 0)

    def late_phase(k, _):
        for i in (5, 6):
            @pl.when(k == i)
            def _():
                q_copy(i + 1, 0).wait_recv()
                q_copy(i + 1, 1).wait_recv()

        step(2, k, 5 + (k - 4) % 3)
        return 0

    lax.fori_loop(5, NR, late_phase, 0)
    for t, half, way in ((2, 1, 0), (2, 0, 1), (3, 0, 0), (3, 1, 1)):
        ring(t, half, way).wait_recv()

    scores(3, 1, 0, 0)

    def second_at(j):
        t = (j + 1) // 3
        return (j + 3 * (t % 2) - 3 * (t // 2)) % NR

    def second_phase(j, _):
        k = second_at(j)
        step(3, k, second_at(j + 1))

        @pl.when(j == 1)
        def _():
            depart(0)

        for i in (2, 3, 4):
            @pl.when(j == i)
            def _():
                depart(i - 1)
                depart(i + 8)

        for i in (5, 6, 7):
            @pl.when(j == i)
            def _():
                depart(i + 2)

        return 0

    lax.fori_loop(1, NR + 1, second_phase, 0)
    relay_head1(4)
    relay_head1(5)
    for i in (10, 11, 12):
        arrive(i)
    relay(3, [mine_of(1, 0), came(10), came(11), came(12)])
    depart(13)
    relay_head1(6)

    def page_wait(k, _):
        page_copy(k).wait()
        return 0

    def pool_part(p, state):
        lax.fori_loop(max(1, p * PART), (p + 1) * PART, page_wait, 0)
        if p == 0:
            own_pages.wait()
        rows = pool[p * PART : (p + 1) * PART].reshape(PART * 64, HD)
        found = lax.dot_general(dq, rows, NT, preferred_element_type=F32)
        found = found + pool_bias[:, p * PART * 64 : (p + 1) * PART * 64]
        m, total, weights = weigh(found)
        o = jnp.dot(weights, rows, preferred_element_type=F32)
        both = jnp.maximum(state[0], m)
        old = jnp.exp2(state[0] - both)
        new = jnp.exp2(m - both)
        return both, state[1] * old + total * new, state[2] * old + o * new

    pool_state = (res_m, res_l, res_o)
    for p in POOL_EARLY:
        pool_state = pool_part(p, pool_state)

    def collect(head):
        others = (13, 7, 8, 9) if head == 0 else (0, 4, 5, 6)
        for i in others:
            arrive(i)
        merged, _ = merge([mine_of(0, head)] + [came(i) for i in others])
        for g in range(GROUP):
            lhs[head, :, g * HD : (g + 1) * HD] = merged[:, g * TOK : (g + 1) * TOK].T.astype(BF16)

    core = tp % 2
    side = tp // 2
    sibling = side * 2 + (1 - core)
    across = (1 - side) * 2 + core
    local[9].wait()
    half_width = GROUP * HD

    def first_copy(c):
        if c == CHUNKS:
            return remote(pdec.at[:, 1 - core], rdec, t1_s.at[c], t1_r.at[c], tp=sibling)
        return remote(pbuf.at[c, :, 1 - core], rbuf.at[c], t1_s.at[c], t1_r.at[c], tp=sibling)

    def second_copy(c):
        if c == CHUNKS:
            return remote(sdec, tdec, t2_s.at[c], t2_r.at[c], tp=across)
        return remote(sbuf.at[c], tbuf.at[c], t2_s.at[c], t2_r.at[c], tp=across)

    def second(c):
        first_copy(c).wait_recv()
        if c == CHUNKS:
            sdec[...] = (
                pdec[1 - side, core].astype(F32) + rdec[1 - side].astype(F32)
            ).astype(BF16)
        else:
            sbuf[c] = (
                pbuf[c, 1 - side, core].astype(F32) + rbuf[c, 1 - side].astype(F32)
            ).astype(BF16)
        second_copy(c).start()

    collect(FIRST_HEAD)
    for c in range(CHUNKS):
        weight = wbuf[FIRST_HEAD * half_width : (FIRST_HEAD + 1) * half_width, c * COLS : (c + 1) * COLS]
        pacc[c] = jnp.dot(lhs[FIRST_HEAD], weight, preferred_element_type=F32)
    last = 1 - FIRST_HEAD
    collect(last)
    for c in range(CHUNKS):
        weight = wbuf[last * half_width : (last + 1) * half_width, c * COLS : (c + 1) * COLS]
        part = pacc[c] + jnp.dot(lhs[last], weight, preferred_element_type=F32)
        pbuf[c] = part.astype(BF16).reshape(2, 2, TOK // 4, COLS)
        first_copy(c).start()
        if c > 0:
            second(c - 1)
    second(CHUNKS - 1)

    for p in POOL_LATE:
        pool_state = pool_part(p, pool_state)
    own_m, own_l, own_o = pool_state
    dec = own_o / own_l
    dec = jnp.concatenate([dec[h * 16 : (h + 1) * 16] for h in range(8)], axis=1).astype(BF16)
    dec_parts = [
        jnp.dot(dec, wbuf[:, c * COLS : (c + 1) * COLS], preferred_element_type=F32)
        for c in range(CHUNKS)
    ]
    for t in range(4):
        rows = jnp.concatenate([part[t * 4 : (t + 1) * 4] for part in dec_parts], axis=0)
        pdec[t // 2, t % 2] = rows.astype(BF16)
    first_copy(CHUNKS).start()
    for c in range(CHUNKS):
        second_copy(c).wait_recv()
        out_ref[:, c * COLS : (c + 1) * COLS] = (
            pbuf[c, side, core].astype(F32) + rbuf[c, side].astype(F32) + tbuf[c].astype(F32)
        ).astype(BF16)
        if c == 1:
            second(CHUNKS)
    second_copy(CHUNKS).wait_recv()
    rows = pdec[side, core].astype(F32) + rdec[side].astype(F32) + tdec[...].astype(F32)
    dout_ref[0] = jnp.concatenate(
        [rows[c * 4 : (c + 1) * 4] for c in range(CHUNKS)], axis=1
    ).astype(BF16)

    for t in range(4):
        for half in range(2):
            for way in range(2):
                if t < 3 or half == way:
                    ring(t, half, way).wait_send()
    for k in range(1, NR):
        for head in range(2):
            q_copy(k, head).wait_send()
    for i in range(MESSAGES):
        for copy in messages(i):
            copy.wait_send()
    for c in range(CHUNKS + 1):
        first_copy(c).wait_send()
        second_copy(c).wait_send()


def hand_out(out_in, dout_in, out_ref, dout_ref):
    out_ref[...] = out_in[...]
    dout_ref[...] = dout_in[...]


def body(
    span_q, cache_kv, span_kv, span_blocks, parked_pages, page_dest, page_req,
    decode_cache, decode_lengths, decode_q, decode_kv, out_weight,
):
    smem = pl.BlockSpec(memory_space=pltpu.SMEM)
    vmem = pl.BlockSpec(memory_space=pltpu.VMEM)
    hbm = pl.BlockSpec(memory_space=pl.ANY)
    dma = pltpu.SemaphoreType.DMA
    out, dout = pl.pallas_call(
        kernel,
        name="layer",
        out_shape=[
            jax.ShapeDtypeStruct((TOK // 4, CHUNKS * COLS), BF16),
            jax.ShapeDtypeStruct((1, 4, CHUNKS * COLS), BF16),
        ],
        in_specs=[smem] * 2 + [hbm] * 10,
        out_specs=[vmem, vmem],
        scratch_shapes=[
            pltpu.VMEM((8 * TOK, HD), BF16),
            pltpu.VMEM((2, 4 * TOK, HD), BF16),
            pltpu.VMEM((32, 128), jnp.int32),
            pltpu.VMEM((32, 128), jnp.int32),
            pltpu.VMEM((128, HD), BF16),
            pltpu.VMEM((64, HD), BF16),
            pltpu.VMEM((64, 128), jnp.int32),
            pltpu.SMEM((64, 128), jnp.int32),
            pltpu.SMEM((NR * NZ,), F32),
            pltpu.VMEM((4, NZ, 2, HD, HD), BF16),
            pltpu.VMEM((NR, 2, QROWS, HD), BF16),
            pltpu.VMEM((2, MOST_KEYS, QROWS), F32),
            pltpu.VMEM((NR, 2, HD + 8, QROWS), F32),
            pltpu.VMEM((NR, 2, 8, QROWS), F32),
            pltpu.VMEM((NR, 2, HD, QROWS), BF16),
            pltpu.VMEM((MESSAGES, HD, QROWS), BF16),
            pltpu.VMEM((NR, 2, 8, TOK), F32),
            pltpu.VMEM((MESSAGES, 8, TOK), F32),
            pltpu.VMEM((4, HD, QROWS), BF16),
            pltpu.VMEM((4, 8, TOK), F32),
            pltpu.VMEM((64, PAGE_ROWS, HD), BF16),
            pltpu.VMEM((64, 2 * PAGE_ROWS, HD), BF16),
            pltpu.VMEM((64, 2 * PAGE_ROWS, HD), BF16),
            pltpu.VMEM((128, POOL), F32),
            pltpu.VMEM((4 * 2048, HD), BF16),
            pltpu.VMEM((8 * HD, CHUNKS * COLS), BF16),
            pltpu.VMEM((2, TOK, GROUP * HD), BF16),
            pltpu.VMEM((CHUNKS, TOK, COLS), F32),
            pltpu.VMEM((CHUNKS, 2, 2, TOK // 4, COLS), BF16),
            pltpu.VMEM((CHUNKS, 2, TOK // 4, COLS), BF16),
            pltpu.VMEM((CHUNKS, TOK // 4, COLS), BF16),
            pltpu.VMEM((CHUNKS, TOK // 4, COLS), BF16),
            pltpu.VMEM((2, 2, 16, COLS), BF16),
            pltpu.VMEM((2, 16, COLS), BF16),
            pltpu.VMEM((16, COLS), BF16),
            pltpu.VMEM((16, COLS), BF16),
            dma((12,)),
            dma((2, 4, 2)), dma((2, 4, 2)),
            dma((NR, 2)), dma((NR, 2)),
            dma((MESSAGES,)), dma((MESSAGES,)),
            dma((MESSAGES,)), dma((MESSAGES,)),
            dma((64,)), dma((64,)),
            dma((CHUNKS + 1,)), dma((CHUNKS + 1,)),
            dma((CHUNKS + 1,)), dma((CHUNKS + 1,)),
        ],
        compiler_params=pltpu.CompilerParams(
            collective_id=0, has_side_effects=True, vmem_limit_bytes=56 << 20
        ),
    )(
        span_blocks, decode_lengths, span_q.reshape(8 * TOK, HD),
        cache_kv.reshape(4 * TOK, HD), span_kv.reshape(4 * TOK, HD),
        parked_pages.reshape(64, PAGE_ROWS, HD), page_dest.reshape(32, 128), page_req.reshape(32, 128),
        decode_cache.reshape(4 * 2048, HD), decode_q.reshape(128, HD), decode_kv.reshape(64, HD),
        out_weight.reshape(8 * HD, CHUNKS * COLS),
    )
    return pl.pallas_call(
        hand_out,
        name="results",
        out_shape=[jax.ShapeDtypeStruct(a.shape, a.dtype) for a in (out, dout)],
        in_specs=[vmem, vmem],
        out_specs=[vmem, vmem],
        compiler_params=pltpu.CompilerParams(vmem_limit_bytes=56 << 20),
    )(out, dout)


def solution(mesh):
    return jax.shard_map(
        body,
        mesh=mesh,
        in_specs=(
            P("ctx", "tp", None),
            P("ctx", "tp", None, None),
            P("ctx", "tp", None, None),
            P(),
            P("ctx", None, "tp", None, None),
            P(),
            P(),
            P("ctx", None, "tp", None, None),
            P("ctx"),
            P("ctx", None, "tp", None),
            P("ctx", None, "tp", None, None),
            P("tp", None, None),
        ),
        out_specs=(P(("ctx", "tp"), None), P(("ctx", "tp"), None, None)),
        check_vma=False,
    )
```
